32 devices in a mesh: cuts: 4 (over z), gx: 2 (over x), gy: 4 (over y, core).
Axes of the slice: x: 2, y: 2, z: 4, core: 2. Of those that a mesh axis runs over, the one named last changes fastest.
Arguments:
- start_heads: float32 [4, 32, 8, 1024], P('cuts', None, 'gx', 'gy'), may hold values from -4 to -0.3
- soil_class: int32 [8, 1024], P('gx', 'gy'), may hold values from 0 to 11
- soil_conductivity: float32 [12], replicated, may hold values from 0.005 to 0.025
- soil_entry: float32 [12], replicated, may hold values from 0.5 to 3
- soil_shape: float32 [12], replicated, may hold values from 1.4 to 2.6
- soil_porosity: float32 [12], replicated, may hold values from 0.25 to 0.45
- emitter_cell: int32 [2048], P(('gx', 'gy')), may hold values from 0 to 1023
- emitter_plan: int32 [2048], P(('gx', 'gy')), may hold values from 0 to 15
- plan_rates: float32 [16, 4], replicated, may hold values from 0.05 to 0.5
Outputs:
- end_heads: float32 [4, 32, 8, 1024], P('cuts', None, 'gx', 'gy')
The draws below stay inside these ranges and needn't reach their ends.
All inputs are finite; a program needn't handle non-finite values.
Results may differ from the reference program's by a relative error of at most 0.0001.
Values sent between devices are 32-bit elements; how exact they have to be, the bound alone decides.
A program may use at most 64 MiB of HBM per device.

```python
import math
import jax
import jax.numpy as jnp

CX = 4
CY = 256
NZ = 32
E_DEV = 256
NSOIL = 12
NSCHED = 16
FINE_STEPS = 4
COARSE_STEPS = 2
SLICES = 4
NX = 8
NY = 1024
EMITTERS = 2048
N_GY = 4


def with_ends(result, rng, smallest, high):
    place = [jax.random.randint(jax.random.fold_in(rng, axis), (), 0, length) for axis, length in enumerate(result.shape)]
    widest = result.shape.index(max(result.shape))
    beside = place[:widest] + [(place[widest] + 1) % result.shape[widest]] + place[widest + 1:]
    return result.at[tuple(place)].set(smallest).at[tuple(beside)].set(high)


def level_of(rng, shape, pieces, least, top_value):
    level = 1.0
    for dim, shards_of in pieces:
        draws = jax.random.uniform(jax.random.fold_in(jax.random.fold_in(rng, 6), dim), (shards_of,), jnp.float32, least / len(pieces), top_value / len(pieces))
        level = level * jnp.repeat(jnp.exp(draws), shape[dim] // shards_of).reshape((-1,) + (1,) * (len(shape) - 1 - dim))
    return level


def setup_inputs(seed: int = 0) -> dict:
    key_list = jax.random.split(jax.random.key(seed), 10)
    start_heads = jnp.clip(-4.0 + 3.7 * jax.random.uniform(key_list[0], (SLICES, NZ, NX, NY), jnp.float32) ** level_of(key_list[0], (SLICES, NZ, NX, NY), ((0, 4), (2, 2), (3, 4)), -0.2, 0.2), -4.0, -0.3)
    soil_class = with_ends(jax.random.randint(key_list[1], (NX, NY), 0, NSOIL), jax.random.fold_in(key_list[1], 1), 0, NSOIL - 1).astype(jnp.int32)
    soil_conductivity = jnp.clip(jnp.exp(jax.random.uniform(key_list[2], (NSOIL,), jnp.float32, math.log(0.005), math.log(0.025))), 0.005, 0.025)
    soil_entry = jnp.clip(jnp.exp(jax.random.uniform(key_list[3], (NSOIL,), jnp.float32, math.log(0.5), math.log(3.0))), 0.5, 3.0)
    soil_shape = jnp.clip(jax.random.uniform(key_list[4], (NSOIL,), jnp.float32, 1.4, 2.6), 1.4, 2.6)
    soil_porosity = jnp.clip(jax.random.uniform(key_list[5], (NSOIL,), jnp.float32, 0.25, 0.45), 0.25, 0.45)
    emitter_cell = with_ends(jax.random.randint(key_list[6], (EMITTERS,), 0, CX * CY), jax.random.fold_in(key_list[6], 1), 0, (CX * CY) - 1).astype(jnp.int32)
    emitter_plan = with_ends(jax.random.randint(key_list[7], (EMITTERS,), 0, NSCHED), jax.random.fold_in(key_list[7], 1), 0, NSCHED - 1).astype(jnp.int32)
    plan_rates = jnp.clip(jnp.exp(jax.random.uniform(key_list[8], (NSCHED, SLICES), jnp.float32, math.log(0.05), math.log(0.5))), 0.05, 0.5)
    return {"start_heads": start_heads, "soil_class": soil_class, "soil_conductivity": soil_conductivity, "soil_entry": soil_entry, "soil_shape": soil_shape, "soil_porosity": soil_porosity, "emitter_cell": emitter_cell, "emitter_plan": emitter_plan, "plan_rates": plan_rates}


STORAGE = 0.3

def conductivity(heads, saturated, entry_scale, shape_index):
    exponent = 1.0 - 1.0 / shape_index
    suction = jnp.maximum(-heads, 0.0) * entry_scale
    powered = jnp.power(suction, shape_index)
    wetted = powered / (1.0 + powered)
    return saturated * jnp.sqrt(jnp.power(1.0 + powered, -exponent)) * jnp.square(1.0 - jnp.power(wetted, exponent))

def capacity(heads, entry_scale, shape_index, porosity):
    exponent = 1.0 - 1.0 / shape_index
    suction = jnp.maximum(-heads, 0.0) * entry_scale
    powered = jnp.power(suction, shape_index)
    return STORAGE + porosity * exponent * shape_index * entry_scale * jnp.power(suction, shape_index - 1.0) * jnp.power(1.0 + powered, -exponent - 1.0)

def advance(heads, params, source, spacing, interval):
    conduct = conductivity(heads, params[0], params[1], params[2])
    storage_term = capacity(heads, params[1], params[2], params[3])
    inverse = 1.0 / (spacing * spacing)
    flow_x = 0.5 * (conduct[:, 1:, :] + conduct[:, :-1, :]) * (heads[:, 1:, :] - heads[:, :-1, :]) * inverse
    balance_x = jnp.pad(flow_x, ((0, 0), (0, 1), (0, 0))) - jnp.pad(flow_x, ((0, 0), (1, 0), (0, 0)))
    flow_y = 0.5 * (conduct[:, :, 1:] + conduct[:, :, :-1]) * (heads[:, :, 1:] - heads[:, :, :-1]) * inverse
    balance_y = jnp.pad(flow_y, ((0, 0), (0, 0), (0, 1))) - jnp.pad(flow_y, ((0, 0), (0, 0), (1, 0)))
    downward = 0.5 * (conduct[:-1] + conduct[1:]) * ((heads[:-1] - heads[1:]) / spacing + 1.0)
    inflow = jnp.concatenate([source[None], downward], axis=0)
    outflow = jnp.concatenate([downward, conduct[-1:]], axis=0)
    balance = balance_x + balance_y + (inflow - outflow) / spacing
    return heads + interval * balance / storage_term

def run_steps(heads, params, source, count, spacing, interval):
    for s in range(count):
        heads = advance(heads, params, source, spacing, interval)
    return heads

def restrict(field):
    depth, rows, columns = field.shape
    return field.reshape(depth // 2, 2, rows // 2, 2, columns // 2, 2).mean(axis=(1, 3, 5))

def prolong(field):
    return jnp.repeat(jnp.repeat(jnp.repeat(field, 2, axis=0), 2, axis=1), 2, axis=2)

def coarsen_columns(params):
    count, rows, columns = params.shape
    return params.reshape(count, rows // 2, 2, columns // 2, 2).mean(axis=(2, 4))

def reference(start_heads, soil_class, soil_conductivity, soil_entry, soil_shape, soil_porosity, emitter_cell, emitter_plan, plan_rates):
    table = jnp.stack([soil_conductivity, soil_entry, soil_shape, soil_porosity])
    params = table[:, soil_class]
    coarse_params = coarsen_columns(params)
    tile_index = jnp.arange(EMITTERS, dtype=jnp.int32) // E_DEV
    row_index = tile_index // N_GY * CX + emitter_cell // CY
    column_index = tile_index % N_GY * CY + emitter_cell % CY
    flat_index = (row_index * NY + column_index).astype(jnp.int32)
    results = []
    chained = None
    for k in range(SLICES):
        emitter_rate = plan_rates[emitter_plan, k]
        source = jnp.zeros((NX * NY,), jnp.float32).at[flat_index].add(emitter_rate).reshape(NX, NY)
        coarse_source = coarsen_columns(source[None])[0]
        fine_heads = run_steps(start_heads[k], params, source, FINE_STEPS, 1.0, 1.0)
        coarse_start = restrict(start_heads[k])
        coarse_old = run_steps(coarse_start, coarse_params, coarse_source, COARSE_STEPS, 2.0, 2.0)
        if k == 0:
            chained = coarse_start
        coarse_new = run_steps(chained, coarse_params, coarse_source, COARSE_STEPS, 2.0, 2.0)
        results.append(fine_heads + prolong(coarse_new - coarse_old))
        chained = coarse_new + (restrict(fine_heads) - coarse_old)
    return jnp.stack(results)
```

```python
import functools

import jax
import jax.numpy as jnp
from jax import lax
from jax.experimental import pallas as pl
from jax.experimental.pallas import tpu as pltpu
from jax.sharding import PartitionSpec as P

FINE_STEPS = 4
COARSE_STEPS = 2


STORAGE = 0.3


def with_halo(cells, sides, width):
    for axis, dim in sides:
        count = lax.axis_size(axis)
        ends = count - 1
        head = lax.slice_in_dim(cells, 0, width, axis=dim)
        tail = lax.slice_in_dim(cells, cells.shape[dim] - width, cells.shape[dim], axis=dim)
        cells = jnp.concatenate(
            [
                lax.ppermute(tail, axis, [(i, (i + 1) % count) for i in range(ends)]),
                cells,
                lax.ppermute(head, axis, [((i + 1) % count, i) for i in range(ends)]),
            ],
            axis=dim,
        )
    return cells


def from_behind(array, axis, by):
    length = lax.axis_size(axis)
    pairs = [(i, i + by) for i in range(length) if 0 <= i + by < length]
    return lax.ppermute(array, axis, pairs)


def conductivity(heads, saturated, entry_scale, shape_index):
    exponent = 1.0 - 1.0 / shape_index
    suction = jnp.maximum(-heads, 0.0) * entry_scale
    powered = jnp.power(suction, shape_index)
    wetted = powered / (1.0 + powered)
    return (
        saturated
        * jnp.sqrt(jnp.power(1.0 + powered, -exponent))
        * jnp.square(1.0 - jnp.power(wetted, exponent))
    )


def capacity(heads, entry_scale, shape_index, porosity):
    exponent = 1.0 - 1.0 / shape_index
    suction = jnp.maximum(-heads, 0.0) * entry_scale
    powered = jnp.power(suction, shape_index)
    return STORAGE + porosity * exponent * shape_index * entry_scale * jnp.power(
        suction, shape_index - 1.0
    ) * jnp.power(1.0 + powered, -exponent - 1.0)


def open_faces(rows, columns):
    global_row = lax.axis_index("gx") * rows + jnp.arange(rows, dtype=jnp.int32)
    global_column = lax.axis_index("gy") * columns + jnp.arange(columns, dtype=jnp.int32)
    row_total = lax.axis_size("gx") * rows
    column_total = lax.axis_size("gy") * columns
    return (
        (global_row + 1 < row_total)[None, :, None],
        (global_row > 0)[None, :, None],
        (global_column + 1 < column_total)[None, None, :],
        (global_column > 0)[None, None, :],
    )


def advance_local(
    heads, padded, conduct, conduct_pad, storage_term, source, spacing, interval, faces
):
    row_up, row_down, column_up, column_down = faces
    inverse = 1.0 / (spacing * spacing)
    flow_up = jnp.where(
        row_up,
        0.5 * (conduct + conduct_pad[:, 2:, 1:-1]) * (padded[:, 2:, 1:-1] - heads) * inverse,
        0.0,
    )
    flow_down = jnp.where(
        row_down,
        0.5 * (conduct + conduct_pad[:, :-2, 1:-1]) * (padded[:, :-2, 1:-1] - heads) * inverse,
        0.0,
    )
    balance_x = flow_up + flow_down
    flow_right = jnp.where(
        column_up,
        0.5 * (conduct + conduct_pad[:, 1:-1, 2:]) * (padded[:, 1:-1, 2:] - heads) * inverse,
        0.0,
    )
    flow_left = jnp.where(
        column_down,
        0.5 * (conduct + conduct_pad[:, 1:-1, :-2]) * (padded[:, 1:-1, :-2] - heads) * inverse,
        0.0,
    )
    balance_y = flow_right + flow_left
    downward = 0.5 * (conduct[:-1] + conduct[1:]) * ((heads[:-1] - heads[1:]) / spacing + 1.0)
    inflow = jnp.concatenate([source[None], downward], axis=0)
    outflow = jnp.concatenate([downward, conduct[-1:]], axis=0)
    balance = balance_x + balance_y + (inflow - outflow) / spacing
    return heads + interval * balance / storage_term


def run_steps(heads, params, source, faces, count, spacing, interval, is_fine):
    for s in range(count):
        conduct = conductivity(heads, params[0], params[1], params[2])
        storage_term = capacity(heads, params[1], params[2], params[3])
        stacked = jnp.stack([heads, conduct])
        if is_fine:
            stacked = with_halo(stacked, (("gx", 2), ("gy", 3)), 1)
        else:
            stacked = with_halo(stacked, (("gx", 2), ("gy", 3)), 1)
        padded = stacked[0]
        conduct_pad = stacked[1]
        heads = advance_local(
            heads, padded, conduct, conduct_pad, storage_term, source, spacing, interval, faces
        )
    return heads


def restrict(field):
    depth, rows, columns = field.shape
    return field.reshape(depth // 2, 2, rows // 2, 2, columns // 2, 2).mean(axis=(1, 3, 5))


def prolong(field):
    return jnp.repeat(jnp.repeat(jnp.repeat(field, 2, axis=0), 2, axis=1), 2, axis=2)


def coarsen_columns(params):
    count, rows, columns = params.shape
    return params.reshape(count, rows // 2, 2, columns // 2, 2).mean(axis=(2, 4))


def on_device(
    start_heads,
    soil_class,
    soil_conductivity,
    soil_entry,
    soil_shape,
    soil_porosity,
    emitter_cell,
    emitter_plan,
    plan_rates,
):
    heads_start = start_heads[0]
    depth, rows, columns = heads_start.shape
    table = jnp.stack([soil_conductivity, soil_entry, soil_shape, soil_porosity])
    classes = jnp.arange(table.shape[1], dtype=jnp.int32)
    matches = soil_class[None, :, :] == classes[:, None, None]
    params = jnp.sum(jnp.where(matches[None], table[:, :, None, None], 0.0), axis=1)
    coarse_params = coarsen_columns(params)
    plans = jnp.arange(plan_rates.shape[0], dtype=jnp.int32)
    picks = emitter_plan[:, None] == plans[None, :]
    rates_all = jnp.sum(jnp.where(picks[:, :, None], plan_rates[None], 0.0), axis=1)
    slice_total = rates_all.shape[1]
    sources = (
        jnp.zeros((slice_total, rows * columns), jnp.float32)
        .at[:, emitter_cell]
        .add(rates_all.T)
        .reshape(slice_total, rows, columns)
    )
    coarse_sources = coarsen_columns(sources)
    slice_index = lax.axis_index("cuts")
    slice_count = lax.axis_size("cuts")
    source = sources[slice_index]
    coarse_source = coarse_sources[slice_index]
    fine_open = open_faces(rows, columns)
    coarse_open = open_faces(rows // 2, columns // 2)
    fine_heads = run_steps(heads_start, params, source, fine_open, FINE_STEPS, 1.0, 1.0, True)

    def coarse_run(current, coarse_src):
        return run_steps(
            current, coarse_params, coarse_src, coarse_open, COARSE_STEPS, 2.0, 2.0, False
        )

    coarse_start = restrict(heads_start)
    coarse_old = coarse_run(coarse_start, coarse_source)
    correction = restrict(fine_heads) - coarse_old
    current = coarse_start
    coarse_new = coarse_old
    for s in range(slice_count):
        coarse_new = coarse_run(current, coarse_source)
        if s + 1 < slice_count:
            arrived = from_behind(coarse_new + correction, "cuts", 1)
            current = jnp.where(slice_index == 0, coarse_start, arrived)
    end_state = fine_heads + prolong(coarse_new - coarse_old)
    return end_state[None]


MESH = pl.DeviceIdType.MESH
EXTRA = 128


def closure(heads, entry, power, half_exponent, half_saturated, gain, interval):
    suction = jnp.maximum(-heads, 0.0) * entry
    lifted = jnp.exp(power * jnp.log(jnp.maximum(suction, 1e-37)))
    grown = 1.0 + suction * lifted
    root = jnp.exp(half_exponent * jnp.log(grown))
    wetted = lifted * root * root
    dry = 1.0 - wetted
    half_conduct = half_saturated * root * dry * dry
    rate = interval * grown / (STORAGE * grown + gain * wetted)
    return half_conduct, rate


def derived(saturated, entry, shape_index, porosity):
    power = shape_index - 1.0
    return (
        entry,
        power,
        -0.5 * power / shape_index,
        0.5 * saturated,
        porosity * power * entry,
    )


def shifted(array, by, axis):
    return pltpu.roll(array, by % array.shape[axis], axis)


def vertical(heads, half, source, spacing):
    depth = heads.shape[0]
    place = lax.broadcasted_iota(jnp.int32, heads.shape, 0)
    below = shifted(heads, -1, 0)
    flow = (half + shifted(half, -1, 0)) * ((heads - below) * (1.0 / spacing) + 1.0)
    outflow = jnp.where(place == depth - 1, 2.0 * half, flow)
    inflow = jnp.where(place == 0, source, shifted(outflow, 1, 0))
    return (inflow - outflow) * (1.0 / spacing)


def coarse_steps(own, other, params, steps, column_open, even):
    wide = 2.0
    pairs = [own, other]
    for s in range(steps):
        closed = [
            closure(pairs[w], *params[w][:5], wide) for w in range(2)
        ]
        across = jnp.where(
            even, 0.0, (closed[0][0] + closed[1][0]) * (pairs[1] - pairs[0])
        )
        fresh = []
        for w in range(2):
            if w == 1 and s == steps - 1:
                fresh.append(pairs[1])
                continue
            heads, (half, rate) = pairs[w], closed[w]
            right = column_open * (half + shifted(half, -2, 1)) * (shifted(heads, -2, 1) - heads)
            lateral = right - shifted(right, 2, 1)
            twin = jnp.where(even, shifted(heads, -1, 1), shifted(heads, 1, 1))
            twin_half = jnp.where(even, shifted(half, -1, 1), shifted(half, 1, 1))
            lateral = lateral + (half + twin_half) * (twin - heads)
            lateral = lateral + across if w == 0 else lateral - across
            balance = lateral * (1.0 / (wide * wide)) + vertical(heads, half, params[w][5], wide)
            fresh.append(heads + rate * balance)
        pairs = fresh
    return pairs[0]


def pair_kernel(
    sizes,
    width,
    heads_ref,
    class_ref,
    saturated_ref,
    entry_ref,
    shape_ref,
    porosity_ref,
    cell_ref,
    plan_ref,
    rates_ref,
    out_ref,
    field,
    halves,
    speeds,
    table,
    coarse_table,
    aux_out,
    aux_in,
    edge_out,
    edge_in,
    fold,
    old,
    fresh,
    correction,
    chain_out,
    chain_in,
    row_send,
    row_recv,
    aux_send,
    aux_recv,
    edge_send,
    edge_recv,
    chain_send,
    chain_recv,
):
    slices, column_tiles = sizes["cuts"], sizes["gy"]
    _, depth, rows, columns = heads_ref.shape
    span = columns + EXTRA
    k = lax.axis_index("cuts")
    gx = lax.axis_index("gx")
    gy = lax.axis_index("gy")
    low = gx == 0
    has_left, has_right = gy > 0, gy < column_tiles - 1
    has_before, has_after = k > 0, k < slices - 1
    pieces = 128 // width

    partner = (k, 1 - gx, gy)
    greeted = (
        (None, partner),
        (has_left, (k, gx, gy - 1)),
        (has_left, (k, 1 - gx, gy - 1)),
        (has_right, (k, gx, gy + 1)),
        (has_right, (k, 1 - gx, gy + 1)),
        (has_before, (k - 1, gx, gy)),
        (has_before, (k - 1, 1 - gx, gy)),
        (has_after, (k + 1, gx, gy)),
        (has_after, (k + 1, 1 - gx, gy)),
    )
    barrier = pltpu.get_barrier_semaphore()
    for there, device in greeted:
        def greet(device=device):
            pl.semaphore_signal(barrier, inc=1, device_id=device, device_id_type=MESH)

        if there is None:
            greet()
        else:
            pl.when(there)(greet)

    own = [heads_ref[0, :, r, :] for r in range(rows)]
    for j in range(rows):
        field[0, j, :, pl.ds(0, columns)] = jnp.where(low, own[j], own[rows - 1 - j])
    classes = class_ref[...].astype(jnp.float32)
    for j in range(rows):
        aux_out[pl.ds(j, 1), :] = jnp.where(
            low, classes[j : j + 1], classes[rows - 1 - j : rows - j]
        )

    kinds = rates_ref.shape[0]
    picked = lax.broadcasted_iota(jnp.int32, rates_ref.shape, 1) == k
    rate_of = jnp.sum(jnp.where(picked, rates_ref[...], 0.0), axis=1, keepdims=True)
    plan = plan_ref[...]
    cell = cell_ref[...]
    count = plan.shape[1]
    planned = plan == lax.broadcasted_iota(jnp.int32, (kinds, count), 0)
    rates = jnp.sum(jnp.where(planned, rate_of, 0.0), axis=0, keepdims=True)
    row_of, column_of = cell // columns, cell % columns
    line = lax.broadcasted_iota(jnp.int32, (8, count), 0)
    line = jnp.where(low, line, rows - 1 - line)
    by_row = jnp.where(row_of == line, rates, 0.0)
    by_column = jnp.where(
        column_of == lax.broadcasted_iota(jnp.int32, (columns, count), 0), 1.0, 0.0
    )
    source = lax.dot_general(
        by_row,
        by_column,
        (((1,), (1,)), ((), ())),
        precision=lax.Precision.HIGHEST,
        preferred_element_type=jnp.float32,
    )
    aux_out[pl.ds(rows, rows), :] = source[:rows]

    lane = lax.broadcasted_iota(jnp.int32, (width, EXTRA), 1)
    packs = [jnp.zeros((width, EXTRA), jnp.float32) for _ in range(2)]
    per_row = depth // width
    for p in range(pieces):
        j, part = p // per_row, p % per_row
        here = (lane >= p * width) & (lane < (p + 1) * width)
        for side in range(2):
            block = field[0, j, pl.ds(part * width, width), pl.ds(side * (columns - 128), 128)]
            packs[side] = jnp.where(here, shifted(block, (p + side) * width, 1), packs[side])
    for side in range(2):
        edge_out[side, pl.ds(0, width), :] = packs[side]
        edge_out[side, pl.ds(width, 8), :] = aux_out[:, pl.ds(side * (columns - 128), 128)]

    def fill(side):
        for who in range(2):
            edge_in[side, who] = edge_out[side]

    pl.when(jnp.logical_not(has_right))(lambda: fill(0))
    pl.when(jnp.logical_not(has_left))(lambda: fill(1))

    sides = [has_left, has_right, has_before, has_after]
    pl.semaphore_wait(barrier, 1 + 2 * sum(there.astype(jnp.int32) for there in sides))

    def copy(source_ref, target_ref, send, recv, device):
        return pltpu.make_async_remote_copy(
            src_ref=source_ref,
            dst_ref=target_ref,
            send_sem=send,
            recv_sem=recv,
            device_id=device,
            device_id_type=MESH,
        )

    row_copies = [
        copy(
            field.at[0, j, :, pl.ds(0, columns)],
            field.at[0, 2 * rows - 1 - j, :, pl.ds(0, columns)],
            row_send.at[j],
            row_recv.at[j],
            partner,
        )
        for j in range(rows)
    ]
    aux_copy = copy(aux_out, aux_in, aux_send, aux_recv, partner)
    edge_copies = [
        [
            copy(
                edge_out.at[side],
                edge_in.at[side, who],
                edge_send.at[side, who],
                edge_recv.at[side, who],
                (k, gx if who == 0 else 1 - gx, gy - 1 if side == 0 else gy + 1),
            )
            for who in range(2)
        ]
        for side in range(2)
    ]
    sends_to = (has_left, has_right)
    hears_from = (has_right, has_left)
    for side in range(2):
        @pl.when(sends_to[side])
        def _():
            for who in range(2):
                edge_copies[side][who].start()
    aux_copy.start()
    for j in reversed(range(rows)):
        row_copies[j].start()

    for side in range(2):
        @pl.when(hears_from[side])
        def _():
            for who in range(2):
                edge_copies[side][who].wait_recv()
    aux_copy.wait_recv()

    third = lax.broadcasted_iota(jnp.int32, (width, EXTRA), 1)
    for who in range(2):
        for p in range(pieces):
            j, part = p // per_row, p % per_row
            from_right = shifted(edge_in[0, who, pl.ds(0, width), :], -p * width, 1)
            from_left = shifted(edge_in[1, who, pl.ds(0, width), :], -(p + 1) * width, 1)
            block = jnp.where(
                third < width, from_right, jnp.where(third >= EXTRA - width, from_left, -1.0)
            )
            row = j if who == 0 else 2 * rows - 1 - j
            field[0, row, pl.ds(part * width, width), pl.ds(columns, EXTRA)] = block

    third8 = lax.broadcasted_iota(jnp.int32, (8, EXTRA), 1)
    wide_aux = [
        jnp.concatenate(
            [
                (aux_out if who == 0 else aux_in)[...],
                jnp.where(
                    third8 < EXTRA // 2,
                    edge_in[0, who, pl.ds(width, 8), :],
                    edge_in[1, who, pl.ds(width, 8), :],
                ),
            ],
            axis=1,
        )
        for who in range(2)
    ]
    lanes = lax.broadcasted_iota(jnp.int32, (1, span), 1)
    even = lanes % 2 == 0
    column = gy * columns + jnp.where(lanes < columns + EXTRA // 2, lanes, lanes - span)
    total = column_tiles * columns
    fine_open = jnp.where((column >= 0) & (column + 1 < total), 1.0, 0.0)
    coarse_open = jnp.where((column >= 0) & (column + 2 < total), 1.0, 0.0)

    def paired(first, second):
        return jnp.where(even, first + shifted(first, -1, 1), second + shifted(second, 1, 1))

    refs = (saturated_ref, entry_ref, shape_ref, porosity_ref)
    for who in range(2):
        cls = wide_aux[who]
        found = [jnp.zeros_like(cls) for _ in refs]
        for c in range(saturated_ref.shape[0]):
            match = cls == float(c)
            found = [jnp.where(match, ref[c], f) for ref, f in zip(refs, found)]
        src = wide_aux[who]
        means = [
            0.25 * paired(f[0:1] + f[1:2], f[2:3] + f[3:4]) for f in found
        ]
        spread = 0.25 * paired(
            src[rows : rows + 1] + src[rows + 1 : rows + 2],
            src[rows + 2 : rows + 3] + src[rows + 3 : rows + 4],
        )
        for i, value in enumerate(derived(*means) + (spread,)):
            coarse_table[who, pl.ds(i, 1), :] = value
        for i, value in enumerate(derived(*[f[:rows] for f in found]) + (src[rows:],)):
            for j in range(rows):
                row = j if who == 0 else 2 * rows - 1 - j
                table[row, pl.ds(i, 1), :] = value[j : j + 1]

    def coarse_params(who):
        return [coarse_table[who, pl.ds(i, 1), :] for i in range(6)]

    def restricted(slot, row_ids):
        for q in range(2):
            total = field[slot, row_ids[2 * q]] + field[slot, row_ids[2 * q + 1]]
            for c in range(span // 128):
                fold[q, c] = total[:, c * 128 : (c + 1) * 128]
        sums = []
        for q in range(2):
            lines = [
                fold[q, c, pl.ds(0, depth // 2, stride=2), :]
                + fold[q, c, pl.ds(1, depth // 2, stride=2), :]
                for c in range(span // 128)
            ]
            sums.append(jnp.concatenate(lines, axis=1))
        return 0.125 * paired(*sums)

    for j in reversed(range(rows)):
        row_copies[j].wait_recv()

    last = 2 * rows - 1
    old[...] = coarse_steps(
        restricted(0, (0, 1, 2, 3)),
        restricted(0, (last, last - 1, last - 2, last - 3)),
        [coarse_params(0), coarse_params(1)],
        COARSE_STEPS,
        coarse_open,
        even,
    )

    for j in range(rows):
        row_copies[j].wait_send()

    for s in range(FINE_STEPS):
        now, later = s % 2, (s + 1) % 2
        reach = 2 * rows - 1 - s

        def close(j, carry):
            given = [table[j, pl.ds(i, 1), :] for i in range(5)]
            half, rate = closure(field[now, j], *given, 1.0)
            halves[j] = half
            speeds[j] = rate
            return carry

        lax.fori_loop(0, reach + 1, close, 0)

        def move(j, carry):
            heads, half = field[now, j], halves[j]
            right = fine_open * (half + shifted(half, -1, 1)) * (shifted(heads, -1, 1) - heads)
            up = (half + halves[j + 1]) * (field[now, j + 1] - heads)
            before = jnp.maximum(j - 1, 0)
            down = (half + halves[before]) * (field[now, before] - heads)
            balance = (
                right
                - shifted(right, 1, 1)
                + up
                + down
                + vertical(heads, half, table[j, pl.ds(5, 1), :], 1.0)
            )
            field[later, j] = heads + speeds[j] * balance
            return carry

        lax.fori_loop(0, reach, move, 0)

    done = FINE_STEPS % 2
    correction[...] = restricted(done, (0, 1, 2, 3)) - old[...]

    chain_copies = [
        copy(
            chain_out,
            chain_in.at[who],
            chain_send.at[who],
            chain_recv.at[who],
            (k + 1, gx if who == 0 else 1 - gx, gy),
        )
        for who in range(2)
    ]

    @pl.when(jnp.logical_not(has_before))
    def _():
        fresh[...] = old[...]

    @pl.when(has_before)
    def _():
        for who in range(2):
            chain_copies[who].wait_recv()
        fresh[...] = coarse_steps(
            chain_in[0],
            chain_in[1],
            [coarse_params(0), coarse_params(1)],
            COARSE_STEPS,
            coarse_open,
            even,
        )

    @pl.when(has_after)
    def _():
        chain_out[...] = fresh[...] + correction[...]
        for who in range(2):
            chain_copies[who].start()

    change = fresh[...] - old[...]
    spread_rows = (
        jnp.where(even, change, shifted(change, 1, 1)),
        jnp.where(even, shifted(change, -1, 1), change),
    )
    for q in range(2):
        for half in range(2):
            for c in range(columns // 128):
                fold[q, c, pl.ds(half, depth // 2, stride=2), :] = spread_rows[q][
                    :, c * 128 : (c + 1) * 128
                ]
    ends = [
        field[done, j, :, pl.ds(0, columns)]
        + jnp.concatenate([fold[j // 2, c] for c in range(columns // 128)], axis=1)
        for j in range(rows)
    ]
    for j in range(rows):
        out_ref[j] = jnp.where(low, ends[j], ends[rows - 1 - j])

    aux_copy.wait_send()
    for side in range(2):
        @pl.when(sends_to[side])
        def _():
            for who in range(2):
                edge_copies[side][who].wait_send()

    @pl.when(has_after)
    def _():
        for who in range(2):
            chain_copies[who].wait_send()


def on_pair(
    sizes,
    start_heads,
    soil_class,
    soil_conductivity,
    soil_entry,
    soil_shape,
    soil_porosity,
    emitter_cell,
    emitter_plan,
    plan_rates,
):
    _, depth, rows, columns = start_heads.shape
    span = columns + EXTRA
    width = 4 * sizes["cuts"]
    vmem = pl.BlockSpec(memory_space=pltpu.VMEM)
    smem = pl.BlockSpec(memory_space=pltpu.SMEM)
    dma = pltpu.SemaphoreType.DMA
    f32 = jnp.float32
    half = (depth // 2, span)
    ends = pl.pallas_call(
        functools.partial(pair_kernel, dict(sizes), width),
        out_shape=jax.ShapeDtypeStruct((rows, depth, columns), f32),
        in_specs=[vmem, vmem, smem, smem, smem, smem, vmem, vmem, vmem],
        out_specs=vmem,
        scratch_shapes=[
            pltpu.VMEM((2, 2 * rows, depth, span), f32),
            pltpu.VMEM((2 * rows, depth, span), f32),
            pltpu.VMEM((2 * rows, depth, span), f32),
            pltpu.VMEM((2 * rows, 8, span), f32),
            pltpu.VMEM((2, 8, span), f32),
            pltpu.VMEM((2 * rows, columns), f32),
            pltpu.VMEM((2 * rows, columns), f32),
            pltpu.VMEM((2, width + 8, EXTRA), f32),
            pltpu.VMEM((2, 2, width + 8, EXTRA), f32),
            pltpu.VMEM((2, span // 128, depth, 128), f32),
            pltpu.VMEM(half, f32),
            pltpu.VMEM(half, f32),
            pltpu.VMEM(half, f32),
            pltpu.VMEM(half, f32),
            pltpu.VMEM((2,) + half, f32),
            dma((rows,)),
            dma((rows,)),
            dma,
            dma,
            dma((2, 2)),
            dma((2, 2)),
            dma((2,)),
            dma((2,)),
        ],
        compiler_params=pltpu.CompilerParams(
            collective_id=0, has_side_effects=True, vmem_limit_bytes=32 * 1024 * 1024
        ),
    )(
        start_heads,
        soil_class,
        soil_conductivity,
        soil_entry,
        soil_shape,
        soil_porosity,
        emitter_cell.reshape(1, -1),
        emitter_plan.reshape(1, -1),
        plan_rates,
    )
    return ends.transpose(1, 0, 2)[None]


def solution(mesh):
    in_specs = (
        P("cuts", None, "gx", "gy"),
        P("gx", "gy"),
        P(),
        P(),
        P(),
        P(),
        P(("gx", "gy")),
        P(("gx", "gy")),
        P(),
    )
    out_specs = P("cuts", None, "gx", "gy")
    sizes = mesh.shape
    fits = sizes["gx"] == 2 and sizes["cuts"] in (4, 8)
    body = functools.partial(on_pair, sizes) if fits else on_device
    return jax.shard_map(
        body, mesh=mesh, in_specs=in_specs, out_specs=out_specs, check_vma=False
    )
```

```python
import functools

import jax
import jax.numpy as jnp
from jax import lax
from jax.experimental import pallas as pl
from jax.experimental.pallas import tpu as pltpu
from jax.sharding import PartitionSpec as P

FINE_STEPS = 4
COARSE_STEPS = 2


STORAGE = 0.3


def with_halo(cells, sides, width):
    for axis, dim in sides:
        count = lax.axis_size(axis)
        ends = count - 1
        head = lax.slice_in_dim(cells, 0, width, axis=dim)
        tail = lax.slice_in_dim(cells, cells.shape[dim] - width, cells.shape[dim], axis=dim)
        cells = jnp.concatenate(
            [
                lax.ppermute(tail, axis, [(i, (i + 1) % count) for i in range(ends)]),
                cells,
                lax.ppermute(head, axis, [((i + 1) % count, i) for i in range(ends)]),
            ],
            axis=dim,
        )
    return cells


def from_behind(array, axis, by):
    length = lax.axis_size(axis)
    pairs = [(i, i + by) for i in range(length) if 0 <= i + by < length]
    return lax.ppermute(array, axis, pairs)


def conductivity(heads, saturated, entry_scale, shape_index):
    exponent = 1.0 - 1.0 / shape_index
    suction = jnp.maximum(-heads, 0.0) * entry_scale
    powered = jnp.power(suction, shape_index)
    wetted = powered / (1.0 + powered)
    return (
        saturated
        * jnp.sqrt(jnp.power(1.0 + powered, -exponent))
        * jnp.square(1.0 - jnp.power(wetted, exponent))
    )


def capacity(heads, entry_scale, shape_index, porosity):
    exponent = 1.0 - 1.0 / shape_index
    suction = jnp.maximum(-heads, 0.0) * entry_scale
    powered = jnp.power(suction, shape_index)
    return STORAGE + porosity * exponent * shape_index * entry_scale * jnp.power(
        suction, shape_index - 1.0
    ) * jnp.power(1.0 + powered, -exponent - 1.0)


def open_faces(rows, columns):
    global_row = lax.axis_index("gx") * rows + jnp.arange(rows, dtype=jnp.int32)
    global_column = lax.axis_index("gy") * columns + jnp.arange(columns, dtype=jnp.int32)
    row_total = lax.axis_size("gx") * rows
    column_total = lax.axis_size("gy") * columns
    return (
        (global_row + 1 < row_total)[None, :, None],
        (global_row > 0)[None, :, None],
        (global_column + 1 < column_total)[None, None, :],
        (global_column > 0)[None, None, :],
    )


def advance_local(
    heads, padded, conduct, conduct_pad, storage_term, source, spacing, interval, faces
):
    row_up, row_down, column_up, column_down = faces
    inverse = 1.0 / (spacing * spacing)
    flow_up = jnp.where(
        row_up,
        0.5 * (conduct + conduct_pad[:, 2:, 1:-1]) * (padded[:, 2:, 1:-1] - heads) * inverse,
        0.0,
    )
    flow_down = jnp.where(
        row_down,
        0.5 * (conduct + conduct_pad[:, :-2, 1:-1]) * (padded[:, :-2, 1:-1] - heads) * inverse,
        0.0,
    )
    balance_x = flow_up + flow_down
    flow_right = jnp.where(
        column_up,
        0.5 * (conduct + conduct_pad[:, 1:-1, 2:]) * (padded[:, 1:-1, 2:] - heads) * inverse,
        0.0,
    )
    flow_left = jnp.where(
        column_down,
        0.5 * (conduct + conduct_pad[:, 1:-1, :-2]) * (padded[:, 1:-1, :-2] - heads) * inverse,
        0.0,
    )
    balance_y = flow_right + flow_left
    downward = 0.5 * (conduct[:-1] + conduct[1:]) * ((heads[:-1] - heads[1:]) / spacing + 1.0)
    inflow = jnp.concatenate([source[None], downward], axis=0)
    outflow = jnp.concatenate([downward, conduct[-1:]], axis=0)
    balance = balance_x + balance_y + (inflow - outflow) / spacing
    return heads + interval * balance / storage_term


def run_steps(heads, params, source, faces, count, spacing, interval, is_fine):
    for s in range(count):
        conduct = conductivity(heads, params[0], params[1], params[2])
        storage_term = capacity(heads, params[1], params[2], params[3])
        stacked = jnp.stack([heads, conduct])
        if is_fine:
            stacked = with_halo(stacked, (("gx", 2), ("gy", 3)), 1)
        else:
            stacked = with_halo(stacked, (("gx", 2), ("gy", 3)), 1)
        padded = stacked[0]
        conduct_pad = stacked[1]
        heads = advance_local(
            heads, padded, conduct, conduct_pad, storage_term, source, spacing, interval, faces
        )
    return heads


def restrict(field):
    depth, rows, columns = field.shape
    return field.reshape(depth // 2, 2, rows // 2, 2, columns // 2, 2).mean(axis=(1, 3, 5))


def prolong(field):
    return jnp.repeat(jnp.repeat(jnp.repeat(field, 2, axis=0), 2, axis=1), 2, axis=2)


def coarsen_columns(params):
    count, rows, columns = params.shape
    return params.reshape(count, rows // 2, 2, columns // 2, 2).mean(axis=(2, 4))


def on_device(
    start_heads,
    soil_class,
    soil_conductivity,
    soil_entry,
    soil_shape,
    soil_porosity,
    emitter_cell,
    emitter_plan,
    plan_rates,
):
    heads_start = start_heads[0]
    depth, rows, columns = heads_start.shape
    table = jnp.stack([soil_conductivity, soil_entry, soil_shape, soil_porosity])
    classes = jnp.arange(table.shape[1], dtype=jnp.int32)
    matches = soil_class[None, :, :] == classes[:, None, None]
    params = jnp.sum(jnp.where(matches[None], table[:, :, None, None], 0.0), axis=1)
    coarse_params = coarsen_columns(params)
    plans = jnp.arange(plan_rates.shape[0], dtype=jnp.int32)
    picks = emitter_plan[:, None] == plans[None, :]
    rates_all = jnp.sum(jnp.where(picks[:, :, None], plan_rates[None], 0.0), axis=1)
    slice_total = rates_all.shape[1]
    sources = (
        jnp.zeros((slice_total, rows * columns), jnp.float32)
        .at[:, emitter_cell]
        .add(rates_all.T)
        .reshape(slice_total, rows, columns)
    )
    coarse_sources = coarsen_columns(sources)
    slice_index = lax.axis_index("cuts")
    slice_count = lax.axis_size("cuts")
    source = sources[slice_index]
    coarse_source = coarse_sources[slice_index]
    fine_open = open_faces(rows, columns)
    coarse_open = open_faces(rows // 2, columns // 2)
    fine_heads = run_steps(heads_start, params, source, fine_open, FINE_STEPS, 1.0, 1.0, True)

    def coarse_run(current, coarse_src):
        return run_steps(
            current, coarse_params, coarse_src, coarse_open, COARSE_STEPS, 2.0, 2.0, False
        )

    coarse_start = restrict(heads_start)
    coarse_old = coarse_run(coarse_start, coarse_source)
    correction = restrict(fine_heads) - coarse_old
    current = coarse_start
    coarse_new = coarse_old
    for s in range(slice_count):
        coarse_new = coarse_run(current, coarse_source)
        if s + 1 < slice_count:
            arrived = from_behind(coarse_new + correction, "cuts", 1)
            current = jnp.where(slice_index == 0, coarse_start, arrived)
    end_state = fine_heads + prolong(coarse_new - coarse_old)
    return end_state[None]


MESH = pl.DeviceIdType.MESH
EXTRA = 128


def closure(heads, entry, power, half_exponent, half_saturated, gain, interval):
    suction = jnp.maximum(-heads, 0.0) * entry
    lifted = jnp.exp(power * jnp.log(jnp.maximum(suction, 1e-37)))
    grown = 1.0 + suction * lifted
    root = jnp.exp(half_exponent * jnp.log(grown))
    wetted = lifted * root * root
    dry = 1.0 - wetted
    half_conduct = half_saturated * root * dry * dry
    rate = interval * grown / (STORAGE * grown + gain * wetted)
    return half_conduct, rate


def derived(saturated, entry, shape_index, porosity):
    power = shape_index - 1.0
    return (
        entry,
        power,
        -0.5 * power / shape_index,
        0.5 * saturated,
        porosity * power * entry,
    )


def shifted(array, by, axis):
    return pltpu.roll(array, by % array.shape[axis], axis)


def vertical(heads, half, source, spacing):
    depth = heads.shape[0]
    place = lax.broadcasted_iota(jnp.int32, heads.shape, 0)
    below = shifted(heads, -1, 0)
    flow = (half + shifted(half, -1, 0)) * ((heads - below) * (1.0 / spacing) + 1.0)
    outflow = jnp.where(place == depth - 1, 2.0 * half, flow)
    inflow = jnp.where(place == 0, source, shifted(outflow, 1, 0))
    return (inflow - outflow) * (1.0 / spacing)


def coarse_steps(own, other, params, steps, column_open, even, both=False):
    wide = 2.0
    pairs = [own, other]
    for s in range(steps):
        closed = [
            closure(pairs[w], *params[w][:5], wide) for w in range(2)
        ]
        across = jnp.where(
            even, 0.0, (closed[0][0] + closed[1][0]) * (pairs[1] - pairs[0])
        )
        fresh = []
        for w in range(2):
            if w == 1 and s == steps - 1 and not both:
                fresh.append(pairs[1])
                continue
            heads, (half, rate) = pairs[w], closed[w]
            right = column_open * (half + shifted(half, -2, 1)) * (shifted(heads, -2, 1) - heads)
            lateral = right - shifted(right, 2, 1)
            twin = jnp.where(even, shifted(heads, -1, 1), shifted(heads, 1, 1))
            twin_half = jnp.where(even, shifted(half, -1, 1), shifted(half, 1, 1))
            lateral = lateral + (half + twin_half) * (twin - heads)
            lateral = lateral + across if w == 0 else lateral - across
            balance = lateral * (1.0 / (wide * wide)) + vertical(heads, half, params[w][5], wide)
            fresh.append(heads + rate * balance)
        pairs = fresh
    return pairs if both else pairs[0]


def pair_kernel(
    sizes,
    width,
    heads_ref,
    class_ref,
    saturated_ref,
    entry_ref,
    shape_ref,
    porosity_ref,
    cell_ref,
    plan_ref,
    rates_ref,
    out_ref,
    field,
    halves,
    speeds,
    table,
    coarse_table,
    coarse_source,
    aux_out,
    aux_in,
    edge_out,
    edge_in,
    fold,
    old,
    fresh,
    chained,
    chain_out,
    chain_in,
    row_send,
    row_recv,
    aux_send,
    aux_recv,
    edge_send,
    edge_recv,
    chain_send,
    chain_recv,
):
    slices, column_tiles = sizes["cuts"], sizes["gy"]
    _, depth, rows, columns = heads_ref.shape
    span = columns + EXTRA
    k = lax.axis_index("cuts")
    gx = lax.axis_index("gx")
    gy = lax.axis_index("gy")
    low = gx == 0
    has_left, has_right = gy > 0, gy < column_tiles - 1
    has_before = k > 0
    pieces = 128 // width

    partner = (k, 1 - gx, gy)
    greeted = (
        (None, partner),
        (has_left, (k, gx, gy - 1)),
        (has_left, (k, 1 - gx, gy - 1)),
        (has_right, (k, gx, gy + 1)),
        (has_right, (k, 1 - gx, gy + 1)),
    ) + tuple(
        (None, (lax.rem(k + d, slices), row_half, gy))
        for d in range(1, slices)
        for row_half in (gx, 1 - gx)
    )
    barrier = pltpu.get_barrier_semaphore()
    for there, device in greeted:
        def greet(device=device):
            pl.semaphore_signal(barrier, inc=1, device_id=device, device_id_type=MESH)

        if there is None:
            greet()
        else:
            pl.when(there)(greet)

    own = [heads_ref[0, :, r, :] for r in range(rows)]
    for j in range(rows):
        field[0, j, :, pl.ds(0, columns)] = jnp.where(low, own[j], own[rows - 1 - j])
    classes = class_ref[...].astype(jnp.float32)
    for j in range(rows):
        aux_out[pl.ds(j, 1), :] = jnp.where(
            low, classes[j : j + 1], classes[rows - 1 - j : rows - j]
        )

    kinds = rates_ref.shape[0]
    plan = plan_ref[...]
    cell = cell_ref[...]
    count = plan.shape[1]
    planned = plan == lax.broadcasted_iota(jnp.int32, (kinds, count), 0)
    row_of, column_of = cell // columns, cell % columns
    line = lax.broadcasted_iota(jnp.int32, (slices * rows, count), 0)
    owner, line = line // rows, line % rows
    line = jnp.where(low, line, rows - 1 - line)
    by_row = jnp.zeros((slices * rows, count), jnp.float32)
    for kk in range(slices):
        rate_of = rates_ref[:, kk : kk + 1]
        rates = jnp.sum(jnp.where(planned, rate_of, 0.0), axis=0, keepdims=True)
        by_row = jnp.where(owner == kk, rates, by_row)
    by_row = jnp.where(row_of == line, by_row, 0.0)
    by_column = jnp.where(
        column_of == lax.broadcasted_iota(jnp.int32, (columns, count), 0), 1.0, 0.0
    ).astype(jnp.bfloat16)
    parts, rest = [], by_row
    for _ in range(3):
        parts.append(rest.astype(jnp.bfloat16))
        rest = rest - parts[-1].astype(jnp.float32)
    sources = sum(
        lax.dot_general(
            part,
            by_column,
            (((1,), (1,)), ((), ())),
            preferred_element_type=jnp.float32,
        )
        for part in parts
    )
    source = sources[:rows]
    for kk in range(1, slices):
        source = jnp.where(k == kk, sources[kk * rows : (kk + 1) * rows], source)
    aux_out[pl.ds(rows, rows), :] = source
    even_own = lax.broadcasted_iota(jnp.int32, (1, columns), 1) % 2 == 0
    for kk in range(slices):
        at = [sources[kk * rows + j : kk * rows + j + 1] for j in range(rows)]
        first, second = at[0] + at[1], at[2] + at[3]
        aux_out[pl.ds(2 * rows + kk, 1), :] = 0.25 * jnp.where(
            even_own, first + shifted(first, -1, 1), second + shifted(second, 1, 1)
        )
    if slices < 8:
        aux_out[pl.ds(2 * rows + slices, 8 - slices), :] = jnp.zeros(
            (8 - slices, columns), jnp.float32
        )

    lane = lax.broadcasted_iota(jnp.int32, (width, EXTRA), 1)
    packs = [jnp.zeros((width, EXTRA), jnp.float32) for _ in range(2)]
    per_row = depth // width
    for p in range(pieces):
        j, part = p // per_row, p % per_row
        here = (lane >= p * width) & (lane < (p + 1) * width)
        for side in range(2):
            block = field[0, j, pl.ds(part * width, width), pl.ds(side * (columns - 128), 128)]
            packs[side] = jnp.where(here, shifted(block, (p + side) * width, 1), packs[side])
    for side in range(2):
        edge_out[side, pl.ds(0, width), :] = packs[side]
        edge_out[side, pl.ds(width, 16), :] = aux_out[:, pl.ds(side * (columns - 128), 128)]

    def fill(side):
        for who in range(2):
            edge_in[side, who] = edge_out[side]

    pl.when(jnp.logical_not(has_right))(lambda: fill(0))
    pl.when(jnp.logical_not(has_left))(lambda: fill(1))

    beside = has_left.astype(jnp.int32) + has_right.astype(jnp.int32)
    pl.semaphore_wait(barrier, 2 * slices - 1 + 2 * beside)

    def copy(source_ref, target_ref, send, recv, device):
        return pltpu.make_async_remote_copy(
            src_ref=source_ref,
            dst_ref=target_ref,
            send_sem=send,
            recv_sem=recv,
            device_id=device,
            device_id_type=MESH,
        )

    row_copies = [
        copy(
            field.at[0, j, :, pl.ds(0, columns)],
            field.at[0, 2 * rows - 1 - j, :, pl.ds(0, columns)],
            row_send.at[j],
            row_recv.at[j],
            partner,
        )
        for j in range(rows)
    ]
    aux_copy = copy(aux_out, aux_in, aux_send, aux_recv, partner)
    edge_copies = [
        [
            copy(
                edge_out.at[side],
                edge_in.at[side, who],
                edge_send.at[side, who],
                edge_recv.at[side, who],
                (k, gx if who == 0 else 1 - gx, gy - 1 if side == 0 else gy + 1),
            )
            for who in range(2)
        ]
        for side in range(2)
    ]
    sends_to = (has_left, has_right)
    hears_from = (has_right, has_left)
    for side in range(2):
        @pl.when(sends_to[side])
        def _():
            for who in range(2):
                edge_copies[side][who].start()
    aux_copy.start()
    for j in reversed(range(rows)):
        row_copies[j].start()

    for side in range(2):
        @pl.when(hears_from[side])
        def _():
            for who in range(2):
                edge_copies[side][who].wait_recv()
    aux_copy.wait_recv()

    third = lax.broadcasted_iota(jnp.int32, (width, EXTRA), 1)
    for who in range(2):
        for p in range(pieces):
            j, part = p // per_row, p % per_row
            from_right = shifted(edge_in[0, who, pl.ds(0, width), :], -p * width, 1)
            from_left = shifted(edge_in[1, who, pl.ds(0, width), :], -(p + 1) * width, 1)
            block = jnp.where(
                third < width, from_right, jnp.where(third >= EXTRA - width, from_left, -1.0)
            )
            row = j if who == 0 else 2 * rows - 1 - j
            field[0, row, pl.ds(part * width, width), pl.ds(columns, EXTRA)] = block

    third8 = lax.broadcasted_iota(jnp.int32, (16, EXTRA), 1)
    wide_aux = [
        jnp.concatenate(
            [
                (aux_out if who == 0 else aux_in)[...],
                jnp.where(
                    third8 < EXTRA // 2,
                    edge_in[0, who, pl.ds(width, 16), :],
                    edge_in[1, who, pl.ds(width, 16), :],
                ),
            ],
            axis=1,
        )
        for who in range(2)
    ]
    lanes = lax.broadcasted_iota(jnp.int32, (1, span), 1)
    even = lanes % 2 == 0
    column = gy * columns + jnp.where(lanes < columns + EXTRA // 2, lanes, lanes - span)
    total = column_tiles * columns
    fine_open = jnp.where((column >= 0) & (column + 1 < total), 1.0, 0.0)
    coarse_open = jnp.where((column >= 0) & (column + 2 < total), 1.0, 0.0)

    def paired(first, second):
        return jnp.where(even, first + shifted(first, -1, 1), second + shifted(second, 1, 1))

    refs = (saturated_ref, entry_ref, shape_ref, porosity_ref)
    for who in range(2):
        cls = wide_aux[who]
        found = [jnp.zeros_like(cls) for _ in refs]
        for c in range(saturated_ref.shape[0]):
            match = cls == float(c)
            found = [jnp.where(match, ref[c], f) for ref, f in zip(refs, found)]
        src = wide_aux[who]
        means = [
            0.25 * paired(f[0:1] + f[1:2], f[2:3] + f[3:4]) for f in found
        ]
        coarse_source[who] = src[2 * rows :]
        for i, value in enumerate(derived(*means)):
            coarse_table[who, pl.ds(i, 1), :] = value
        for i, value in enumerate(derived(*[f[:rows] for f in found]) + (src[rows : 2 * rows],)):
            for j in range(rows):
                row = j if who == 0 else 2 * rows - 1 - j
                table[row, pl.ds(i, 1), :] = value[j : j + 1]

    def coarse_params(kk):
        return [
            [coarse_table[who, pl.ds(i, 1), :] for i in range(5)]
            + [coarse_source[who, pl.ds(kk, 1), :]]
            for who in range(2)
        ]

    def restricted(slot, row_ids):
        for q in range(2):
            total = field[slot, row_ids[2 * q]] + field[slot, row_ids[2 * q + 1]]
            for c in range(span // 128):
                fold[q, c] = total[:, c * 128 : (c + 1) * 128]
        sums = []
        for q in range(2):
            lines = [
                fold[q, c, pl.ds(0, depth // 2, stride=2), :]
                + fold[q, c, pl.ds(1, depth // 2, stride=2), :]
                for c in range(span // 128)
            ]
            sums.append(jnp.concatenate(lines, axis=1))
        return 0.125 * paired(*sums)

    for j in reversed(range(rows)):
        row_copies[j].wait_recv()

    last = 2 * rows - 1
    old[...] = coarse_steps(
        restricted(0, (0, 1, 2, 3)),
        restricted(0, (last, last - 1, last - 2, last - 3)),
        coarse_params(k),
        COARSE_STEPS,
        coarse_open,
        even,
    )

    for j in range(rows):
        row_copies[j].wait_send()

    for s in range(FINE_STEPS):
        now, later = s % 2, (s + 1) % 2
        reach = 2 * rows - 1 - s

        def close(j, carry):
            given = [table[j, pl.ds(i, 1), :] for i in range(5)]
            half, rate = closure(field[now, j], *given, 1.0)
            halves[j] = half
            speeds[j] = rate
            return carry

        lax.fori_loop(0, reach + 1, close, 0)

        def move(j, carry):
            heads, half = field[now, j], halves[j]
            right = fine_open * (half + shifted(half, -1, 1)) * (shifted(heads, -1, 1) - heads)
            up = (half + halves[j + 1]) * (field[now, j + 1] - heads)
            before = jnp.maximum(j - 1, 0)
            down = (half + halves[before]) * (field[now, before] - heads)
            balance = (
                right
                - shifted(right, 1, 1)
                + up
                + down
                + vertical(heads, half, table[j, pl.ds(5, 1), :], 1.0)
            )
            field[later, j] = heads + speeds[j] * balance
            return carry

        lax.fori_loop(0, reach, move, 0)

    done = FINE_STEPS % 2
    reached = restricted(done, (0, 1, 2, 3))
    chain_out[...] = (reached - old[...]) + jnp.where(has_before, 0.0, old[...])

    def chain_copy(far, who):
        return copy(
            chain_out,
            chain_in.at[k, who],
            chain_send.at[far - 1, who],
            chain_recv.at[k, who],
            (k + far, gx if who == 0 else 1 - gx, gy),
        )

    def chain_wait(kk):
        for who in range(2):
            copy(
                chain_out,
                chain_in.at[kk, who],
                chain_send.at[0, who],
                chain_recv.at[kk, who],
                partner,
            ).wait_recv()

    for far in reversed(range(1, slices)):
        @pl.when(k + far < slices)
        def _():
            for who in range(2):
                chain_copy(far, who).start()

    for kk in range(slices - 1):
        @pl.when(k > kk)
        def _():
            chain_wait(kk)
            if kk == 0:
                for who in range(2):
                    chained[who] = chain_in[0, who]
            else:
                moved = coarse_steps(
                    chained[0],
                    chained[1],
                    coarse_params(kk),
                    COARSE_STEPS,
                    coarse_open,
                    even,
                    both=True,
                )
                for who in range(2):
                    chained[who] = moved[who] + chain_in[kk, who]

    @pl.when(jnp.logical_not(has_before))
    def _():
        fresh[...] = old[...]

    @pl.when(has_before)
    def _():
        fresh[...] = coarse_steps(
            chained[0], chained[1], coarse_params(k), COARSE_STEPS, coarse_open, even
        )

    change = fresh[...] - old[...]
    spread_rows = (
        jnp.where(even, change, shifted(change, 1, 1)),
        jnp.where(even, shifted(change, -1, 1), change),
    )
    for q in range(2):
        for half in range(2):
            for c in range(columns // 128):
                fold[q, c, pl.ds(half, depth // 2, stride=2), :] = spread_rows[q][
                    :, c * 128 : (c + 1) * 128
                ]
    ends = [
        field[done, j, :, pl.ds(0, columns)]
        + jnp.concatenate([fold[j // 2, c] for c in range(columns // 128)], axis=1)
        for j in range(rows)
    ]
    for j in range(rows):
        out_ref[j] = jnp.where(low, ends[j], ends[rows - 1 - j])

    aux_copy.wait_send()
    for side in range(2):
        @pl.when(sends_to[side])
        def _():
            for who in range(2):
                edge_copies[side][who].wait_send()

    for far in range(1, slices):
        @pl.when(k + far < slices)
        def _():
            for who in range(2):
                chain_copy(far, who).wait_send()


def on_pair(
    sizes,
    start_heads,
    soil_class,
    soil_conductivity,
    soil_entry,
    soil_shape,
    soil_porosity,
    emitter_cell,
    emitter_plan,
    plan_rates,
):
    _, depth, rows, columns = start_heads.shape
    span = columns + EXTRA
    width = 4 * sizes["cuts"]
    vmem = pl.BlockSpec(memory_space=pltpu.VMEM)
    smem = pl.BlockSpec(memory_space=pltpu.SMEM)
    dma = pltpu.SemaphoreType.DMA
    f32 = jnp.float32
    half = (depth // 2, span)
    ends = pl.pallas_call(
        functools.partial(pair_kernel, dict(sizes), width),
        out_shape=jax.ShapeDtypeStruct((rows, depth, columns), f32),
        in_specs=[vmem, vmem, smem, smem, smem, smem, vmem, vmem, vmem],
        out_specs=vmem,
        scratch_shapes=[
            pltpu.VMEM((2, 2 * rows, depth, span), f32),
            pltpu.VMEM((2 * rows, depth, span), f32),
            pltpu.VMEM((2 * rows, depth, span), f32),
            pltpu.VMEM((2 * rows, 8, span), f32),
            pltpu.VMEM((2, 8, span), f32),
            pltpu.VMEM((2, 8, span), f32),
            pltpu.VMEM((16, columns), f32),
            pltpu.VMEM((16, columns), f32),
            pltpu.VMEM((2, width + 16, EXTRA), f32),
            pltpu.VMEM((2, 2, width + 16, EXTRA), f32),
            pltpu.VMEM((2, span // 128, depth, 128), f32),
            pltpu.VMEM(half, f32),
            pltpu.VMEM(half, f32),
            pltpu.VMEM((2,) + half, f32),
            pltpu.VMEM(half, f32),
            pltpu.VMEM((sizes["cuts"], 2) + half, f32),
            dma((rows,)),
            dma((rows,)),
            dma,
            dma,
            dma((2, 2)),
            dma((2, 2)),
            dma((sizes["cuts"], 2)),
            dma((sizes["cuts"], 2)),
        ],
        compiler_params=pltpu.CompilerParams(
            collective_id=0, has_side_effects=True, vmem_limit_bytes=32 * 1024 * 1024
        ),
    )(
        start_heads,
        soil_class,
        soil_conductivity,
        soil_entry,
        soil_shape,
        soil_porosity,
        emitter_cell.reshape(1, -1),
        emitter_plan.reshape(1, -1),
        plan_rates,
    )
    return ends.transpose(1, 0, 2)[None]


def solution(mesh):
    in_specs = (
        P("cuts", None, "gx", "gy"),
        P("gx", "gy"),
        P(),
        P(),
        P(),
        P(),
        P(("gx", "gy")),
        P(("gx", "gy")),
        P(),
    )
    out_specs = P("cuts", None, "gx", "gy")
    sizes = mesh.shape
    fits = sizes["gx"] == 2 and sizes["cuts"] in (4, 8)
    body = functools.partial(on_pair, sizes) if fits else on_device
    return jax.shard_map(
        body, mesh=mesh, in_specs=in_specs, out_specs=out_specs, check_vma=False
    )
```

```python
import functools

import jax
import jax.numpy as jnp
from jax import lax
from jax.experimental import pallas as pl
from jax.experimental.pallas import tpu as pltpu
from jax.sharding import PartitionSpec as P

FINE_STEPS = 4
COARSE_STEPS = 2


STORAGE = 0.3


def with_halo(cells, sides, width):
    for axis, dim in sides:
        count = lax.axis_size(axis)
        ends = count - 1
        head = lax.slice_in_dim(cells, 0, width, axis=dim)
        tail = lax.slice_in_dim(cells, cells.shape[dim] - width, cells.shape[dim], axis=dim)
        cells = jnp.concatenate(
            [
                lax.ppermute(tail, axis, [(i, (i + 1) % count) for i in range(ends)]),
                cells,
                lax.ppermute(head, axis, [((i + 1) % count, i) for i in range(ends)]),
            ],
            axis=dim,
        )
    return cells


def from_behind(array, axis, by):
    length = lax.axis_size(axis)
    pairs = [(i, i + by) for i in range(length) if 0 <= i + by < length]
    return lax.ppermute(array, axis, pairs)


def conductivity(heads, saturated, entry_scale, shape_index):
    exponent = 1.0 - 1.0 / shape_index
    suction = jnp.maximum(-heads, 0.0) * entry_scale
    powered = jnp.power(suction, shape_index)
    wetted = powered / (1.0 + powered)
    return (
        saturated
        * jnp.sqrt(jnp.power(1.0 + powered, -exponent))
        * jnp.square(1.0 - jnp.power(wetted, exponent))
    )


def capacity(heads, entry_scale, shape_index, porosity):
    exponent = 1.0 - 1.0 / shape_index
    suction = jnp.maximum(-heads, 0.0) * entry_scale
    powered = jnp.power(suction, shape_index)
    return STORAGE + porosity * exponent * shape_index * entry_scale * jnp.power(
        suction, shape_index - 1.0
    ) * jnp.power(1.0 + powered, -exponent - 1.0)


def open_faces(rows, columns):
    global_row = lax.axis_index("gx") * rows + jnp.arange(rows, dtype=jnp.int32)
    global_column = lax.axis_index("gy") * columns + jnp.arange(columns, dtype=jnp.int32)
    row_total = lax.axis_size("gx") * rows
    column_total = lax.axis_size("gy") * columns
    return (
        (global_row + 1 < row_total)[None, :, None],
        (global_row > 0)[None, :, None],
        (global_column + 1 < column_total)[None, None, :],
        (global_column > 0)[None, None, :],
    )


def advance_local(
    heads, padded, conduct, conduct_pad, storage_term, source, spacing, interval, faces
):
    row_up, row_down, column_up, column_down = faces
    inverse = 1.0 / (spacing * spacing)
    flow_up = jnp.where(
        row_up,
        0.5 * (conduct + conduct_pad[:, 2:, 1:-1]) * (padded[:, 2:, 1:-1] - heads) * inverse,
        0.0,
    )
    flow_down = jnp.where(
        row_down,
        0.5 * (conduct + conduct_pad[:, :-2, 1:-1]) * (padded[:, :-2, 1:-1] - heads) * inverse,
        0.0,
    )
    balance_x = flow_up + flow_down
    flow_right = jnp.where(
        column_up,
        0.5 * (conduct + conduct_pad[:, 1:-1, 2:]) * (padded[:, 1:-1, 2:] - heads) * inverse,
        0.0,
    )
    flow_left = jnp.where(
        column_down,
        0.5 * (conduct + conduct_pad[:, 1:-1, :-2]) * (padded[:, 1:-1, :-2] - heads) * inverse,
        0.0,
    )
    balance_y = flow_right + flow_left
    downward = 0.5 * (conduct[:-1] + conduct[1:]) * ((heads[:-1] - heads[1:]) / spacing + 1.0)
    inflow = jnp.concatenate([source[None], downward], axis=0)
    outflow = jnp.concatenate([downward, conduct[-1:]], axis=0)
    balance = balance_x + balance_y + (inflow - outflow) / spacing
    return heads + interval * balance / storage_term


def run_steps(heads, params, source, faces, count, spacing, interval, is_fine):
    for s in range(count):
        conduct = conductivity(heads, params[0], params[1], params[2])
        storage_term = capacity(heads, params[1], params[2], params[3])
        stacked = jnp.stack([heads, conduct])
        if is_fine:
            stacked = with_halo(stacked, (("gx", 2), ("gy", 3)), 1)
        else:
            stacked = with_halo(stacked, (("gx", 2), ("gy", 3)), 1)
        padded = stacked[0]
        conduct_pad = stacked[1]
        heads = advance_local(
            heads, padded, conduct, conduct_pad, storage_term, source, spacing, interval, faces
        )
    return heads


def restrict(field):
    depth, rows, columns = field.shape
    return field.reshape(depth // 2, 2, rows // 2, 2, columns // 2, 2).mean(axis=(1, 3, 5))


def prolong(field):
    return jnp.repeat(jnp.repeat(jnp.repeat(field, 2, axis=0), 2, axis=1), 2, axis=2)


def coarsen_columns(params):
    count, rows, columns = params.shape
    return params.reshape(count, rows // 2, 2, columns // 2, 2).mean(axis=(2, 4))


def on_device(
    start_heads,
    soil_class,
    soil_conductivity,
    soil_entry,
    soil_shape,
    soil_porosity,
    emitter_cell,
    emitter_plan,
    plan_rates,
):
    heads_start = start_heads[0]
    depth, rows, columns = heads_start.shape
    table = jnp.stack([soil_conductivity, soil_entry, soil_shape, soil_porosity])
    classes = jnp.arange(table.shape[1], dtype=jnp.int32)
    matches = soil_class[None, :, :] == classes[:, None, None]
    params = jnp.sum(jnp.where(matches[None], table[:, :, None, None], 0.0), axis=1)
    coarse_params = coarsen_columns(params)
    plans = jnp.arange(plan_rates.shape[0], dtype=jnp.int32)
    picks = emitter_plan[:, None] == plans[None, :]
    rates_all = jnp.sum(jnp.where(picks[:, :, None], plan_rates[None], 0.0), axis=1)
    slice_total = rates_all.shape[1]
    sources = (
        jnp.zeros((slice_total, rows * columns), jnp.float32)
        .at[:, emitter_cell]
        .add(rates_all.T)
        .reshape(slice_total, rows, columns)
    )
    coarse_sources = coarsen_columns(sources)
    slice_index = lax.axis_index("cuts")
    slice_count = lax.axis_size("cuts")
    source = sources[slice_index]
    coarse_source = coarse_sources[slice_index]
    fine_open = open_faces(rows, columns)
    coarse_open = open_faces(rows // 2, columns // 2)
    fine_heads = run_steps(heads_start, params, source, fine_open, FINE_STEPS, 1.0, 1.0, True)

    def coarse_run(current, coarse_src):
        return run_steps(
            current, coarse_params, coarse_src, coarse_open, COARSE_STEPS, 2.0, 2.0, False
        )

    coarse_start = restrict(heads_start)
    coarse_old = coarse_run(coarse_start, coarse_source)
    correction = restrict(fine_heads) - coarse_old
    current = coarse_start
    coarse_new = coarse_old
    for s in range(slice_count):
        coarse_new = coarse_run(current, coarse_source)
        if s + 1 < slice_count:
            arrived = from_behind(coarse_new + correction, "cuts", 1)
            current = jnp.where(slice_index == 0, coarse_start, arrived)
    end_state = fine_heads + prolong(coarse_new - coarse_old)
    return end_state[None]


MESH = pl.DeviceIdType.MESH
EXTRA = 128


def closure(heads, entry, power, half_exponent, half_saturated, gain, interval):
    suction = jnp.maximum(-heads, 0.0) * entry
    lifted = jnp.exp(power * jnp.log(jnp.maximum(suction, 1e-37)))
    grown = 1.0 + suction * lifted
    root = jnp.exp(half_exponent * jnp.log(grown))
    wetted = lifted * root * root
    dry = 1.0 - wetted
    half_conduct = half_saturated * root * dry * dry
    rate = interval * grown / (STORAGE * grown + gain * wetted)
    return half_conduct, rate


def derived(saturated, entry, shape_index, porosity):
    power = shape_index - 1.0
    return (
        entry,
        power,
        -0.5 * power / shape_index,
        0.5 * saturated,
        porosity * power * entry,
    )


def shifted(array, by, axis):
    return pltpu.roll(array, by % array.shape[axis], axis)


def vertical(heads, half, source, spacing):
    depth = heads.shape[0]
    place = lax.broadcasted_iota(jnp.int32, heads.shape, 0)
    below = shifted(heads, -1, 0)
    flow = (half + shifted(half, -1, 0)) * ((heads - below) * (1.0 / spacing) + 1.0)
    outflow = jnp.where(place == depth - 1, 2.0 * half, flow)
    inflow = jnp.where(place == 0, source, shifted(outflow, 1, 0))
    return (inflow - outflow) * (1.0 / spacing)


def coarse_steps(own, other, params, steps, column_open, even, both=False):
    wide = 2.0
    pairs = [own, other]
    for s in range(steps):
        closed = [
            closure(pairs[w], *params[w][:5], wide) for w in range(2)
        ]
        across = jnp.where(
            even, 0.0, (closed[0][0] + closed[1][0]) * (pairs[1] - pairs[0])
        )
        fresh = []
        for w in range(2):
            if w == 1 and s == steps - 1 and not both:
                fresh.append(pairs[1])
                continue
            heads, (half, rate) = pairs[w], closed[w]
            right = column_open * (half + shifted(half, -2, 1)) * (shifted(heads, -2, 1) - heads)
            lateral = right - shifted(right, 2, 1)
            twin = jnp.where(even, shifted(heads, -1, 1), shifted(heads, 1, 1))
            twin_half = jnp.where(even, shifted(half, -1, 1), shifted(half, 1, 1))
            lateral = lateral + (half + twin_half) * (twin - heads)
            lateral = lateral + across if w == 0 else lateral - across
            balance = lateral * (1.0 / (wide * wide)) + vertical(heads, half, params[w][5], wide)
            fresh.append(heads + rate * balance)
        pairs = fresh
    return pairs if both else pairs[0]


def pair_kernel(
    sizes,
    width,
    heads_hbm,
    class_hbm,
    saturated_hbm,
    entry_hbm,
    shape_hbm,
    porosity_hbm,
    cell_hbm,
    plan_hbm,
    rates_hbm,
    out_ref,
    class_ref,
    saturated_ref,
    entry_ref,
    shape_ref,
    porosity_ref,
    cell_ref,
    plan_ref,
    rates_ref,
    load_sem,
    field,
    halves,
    speeds,
    table,
    coarse_table,
    coarse_source,
    aux_out,
    aux_in,
    edge_out,
    edge_in,
    fold,
    old,
    fresh,
    chained,
    chain_out,
    chain_in,
    row_send,
    row_recv,
    aux_send,
    aux_recv,
    edge_send,
    edge_recv,
    chain_send,
    chain_recv,
):
    slices, column_tiles = sizes["cuts"], sizes["gy"]
    _, depth, rows, columns = heads_hbm.shape
    span = columns + EXTRA
    k = lax.axis_index("cuts")
    gx = lax.axis_index("gx")
    gy = lax.axis_index("gy")
    low = gx == 0
    has_left, has_right = gy > 0, gy < column_tiles - 1
    has_before = k > 0
    pieces = 128 // width

    partner = (k, 1 - gx, gy)
    greeted = (
        (None, partner),
        (has_left, (k, gx, gy - 1)),
        (has_left, (k, 1 - gx, gy - 1)),
        (has_right, (k, gx, gy + 1)),
        (has_right, (k, 1 - gx, gy + 1)),
    ) + tuple(
        (None, (lax.rem(k + d, slices), row_half, gy))
        for d in range(1, slices)
        for row_half in (gx, 1 - gx)
    )
    barrier = pltpu.get_barrier_semaphore()
    for there, device in greeted:
        def greet(device=device):
            pl.semaphore_signal(barrier, inc=1, device_id=device, device_id_type=MESH)

        if there is None:
            greet()
        else:
            pl.when(there)(greet)

    loads = [
        pltpu.make_async_copy(
            heads_hbm.at[0, :, r, :],
            field.at[0, jnp.where(low, r, rows - 1 - r), :, pl.ds(0, columns)],
            load_sem.at[r],
        )
        for r in range(rows)
    ]
    small = [
        pltpu.make_async_copy(there, here, load_sem.at[rows + i])
        for i, (there, here) in enumerate(
            (
                (class_hbm, class_ref),
                (cell_hbm, cell_ref),
                (plan_hbm, plan_ref),
                (rates_hbm, rates_ref),
                (saturated_hbm, saturated_ref),
                (entry_hbm, entry_ref),
                (shape_hbm, shape_ref),
                (porosity_hbm, porosity_ref),
            )
        )
    ]
    for load in small + loads:
        load.start()
    for load in small:
        load.wait()
    classes = class_ref[...].astype(jnp.float32)
    for j in range(rows):
        aux_out[pl.ds(j, 1), :] = jnp.where(
            low, classes[j : j + 1], classes[rows - 1 - j : rows - j]
        )

    kinds = rates_ref.shape[1]
    plan = plan_ref[...]
    cell = cell_ref[...]
    count = plan.shape[1]
    rates_all = jnp.zeros((slices, count), jnp.float32)
    for kind in range(kinds):
        rates_all = jnp.where(plan == kind, rates_ref[:, kind : kind + 1], rates_all)
    row_of, column_of = cell // columns, cell % columns
    line = lax.broadcasted_iota(jnp.int32, (slices * rows, count), 0)
    owner, line = line // rows, line % rows
    line = jnp.where(low, line, rows - 1 - line)
    by_row = jnp.zeros((slices * rows, count), jnp.float32)
    for kk in range(slices):
        by_row = jnp.where(owner == kk, rates_all[kk : kk + 1], by_row)
    by_row = jnp.where(row_of == line, by_row, 0.0)
    by_column = jnp.where(
        column_of == lax.broadcasted_iota(jnp.int32, (columns, count), 0), 1.0, 0.0
    ).astype(jnp.bfloat16)
    parts, rest = [], by_row
    for _ in range(3):
        parts.append(rest.astype(jnp.bfloat16))
        rest = rest - parts[-1].astype(jnp.float32)
    sources = sum(
        lax.dot_general(
            part,
            by_column,
            (((1,), (1,)), ((), ())),
            preferred_element_type=jnp.float32,
        )
        for part in parts
    )
    source = sources[:rows]
    for kk in range(1, slices):
        source = jnp.where(k == kk, sources[kk * rows : (kk + 1) * rows], source)
    aux_out[pl.ds(rows, rows), :] = source
    even_own = lax.broadcasted_iota(jnp.int32, (1, columns), 1) % 2 == 0
    for kk in range(slices):
        at = [sources[kk * rows + j : kk * rows + j + 1] for j in range(rows)]
        first, second = at[0] + at[1], at[2] + at[3]
        aux_out[pl.ds(2 * rows + kk, 1), :] = 0.25 * jnp.where(
            even_own, first + shifted(first, -1, 1), second + shifted(second, 1, 1)
        )
    if slices < 8:
        aux_out[pl.ds(2 * rows + slices, 8 - slices), :] = jnp.zeros(
            (8 - slices, columns), jnp.float32
        )

    for load in loads:
        load.wait()
    lane = lax.broadcasted_iota(jnp.int32, (width, EXTRA), 1)
    packs = [jnp.zeros((width, EXTRA), jnp.float32) for _ in range(2)]
    per_row = depth // width
    for p in range(pieces):
        j, part = p // per_row, p % per_row
        here = (lane >= p * width) & (lane < (p + 1) * width)
        for side in range(2):
            block = field[0, j, pl.ds(part * width, width), pl.ds(side * (columns - 128), 128)]
            packs[side] = jnp.where(here, shifted(block, (p + side) * width, 1), packs[side])
    for side in range(2):
        edge_out[side, pl.ds(0, width), :] = packs[side]
        edge_out[side, pl.ds(width, 16), :] = aux_out[:, pl.ds(side * (columns - 128), 128)]

    def fill(side):
        for who in range(2):
            edge_in[side, who] = edge_out[side]

    pl.when(jnp.logical_not(has_right))(lambda: fill(0))
    pl.when(jnp.logical_not(has_left))(lambda: fill(1))

    beside = has_left.astype(jnp.int32) + has_right.astype(jnp.int32)
    pl.semaphore_wait(barrier, 2 * slices - 1 + 2 * beside)

    def copy(source_ref, target_ref, send, recv, device):
        return pltpu.make_async_remote_copy(
            src_ref=source_ref,
            dst_ref=target_ref,
            send_sem=send,
            recv_sem=recv,
            device_id=device,
            device_id_type=MESH,
        )

    row_copies = [
        copy(
            field.at[0, j, :, pl.ds(0, columns)],
            field.at[0, 2 * rows - 1 - j, :, pl.ds(0, columns)],
            row_send.at[j],
            row_recv.at[j],
            partner,
        )
        for j in range(rows)
    ]
    aux_copy = copy(aux_out, aux_in, aux_send, aux_recv, partner)
    edge_copies = [
        [
            copy(
                edge_out.at[side],
                edge_in.at[side, who],
                edge_send.at[side, who],
                edge_recv.at[side, who],
                (k, gx if who == 0 else 1 - gx, gy - 1 if side == 0 else gy + 1),
            )
            for who in range(2)
        ]
        for side in range(2)
    ]
    sends_to = (has_left, has_right)
    hears_from = (has_right, has_left)
    for side in range(2):
        @pl.when(sends_to[side])
        def _():
            for who in range(2):
                edge_copies[side][who].start()
    aux_copy.start()
    for j in reversed(range(rows)):
        row_copies[j].start()

    for side in range(2):
        @pl.when(hears_from[side])
        def _():
            for who in range(2):
                edge_copies[side][who].wait_recv()
    aux_copy.wait_recv()

    third = lax.broadcasted_iota(jnp.int32, (width, EXTRA), 1)
    for who in range(2):
        for p in range(pieces):
            j, part = p // per_row, p % per_row
            from_right = shifted(edge_in[0, who, pl.ds(0, width), :], -p * width, 1)
            from_left = shifted(edge_in[1, who, pl.ds(0, width), :], -(p + 1) * width, 1)
            block = jnp.where(
                third < width, from_right, jnp.where(third >= EXTRA - width, from_left, -1.0)
            )
            row = j if who == 0 else 2 * rows - 1 - j
            field[0, row, pl.ds(part * width, width), pl.ds(columns, EXTRA)] = block

    third8 = lax.broadcasted_iota(jnp.int32, (16, EXTRA), 1)
    wide_aux = [
        jnp.concatenate(
            [
                (aux_out if who == 0 else aux_in)[...],
                jnp.where(
                    third8 < EXTRA // 2,
                    edge_in[0, who, pl.ds(width, 16), :],
                    edge_in[1, who, pl.ds(width, 16), :],
                ),
            ],
            axis=1,
        )
        for who in range(2)
    ]
    lanes = lax.broadcasted_iota(jnp.int32, (1, span), 1)
    even = lanes % 2 == 0
    column = gy * columns + jnp.where(lanes < columns + EXTRA // 2, lanes, lanes - span)
    total = column_tiles * columns
    fine_open = jnp.where((column >= 0) & (column + 1 < total), 1.0, 0.0)
    coarse_open = jnp.where((column >= 0) & (column + 2 < total), 1.0, 0.0)

    def paired(first, second):
        return jnp.where(even, first + shifted(first, -1, 1), second + shifted(second, 1, 1))

    refs = (saturated_ref, entry_ref, shape_ref, porosity_ref)
    for who in range(2):
        cls = wide_aux[who]
        found = [jnp.zeros_like(cls) for _ in refs]
        for c in range(saturated_ref.shape[0]):
            match = cls == float(c)
            found = [jnp.where(match, ref[c], f) for ref, f in zip(refs, found)]
        src = wide_aux[who]
        means = [
            0.25 * paired(f[0:1] + f[1:2], f[2:3] + f[3:4]) for f in found
        ]
        coarse_source[who] = src[2 * rows :]
        for i, value in enumerate(derived(*means)):
            coarse_table[who, pl.ds(i, 1), :] = value
        for i, value in enumerate(derived(*[f[:rows] for f in found]) + (src[rows : 2 * rows],)):
            for j in range(rows):
                row = j if who == 0 else 2 * rows - 1 - j
                table[row, pl.ds(i, 1), :] = value[j : j + 1]

    def coarse_params(kk):
        return [
            [coarse_table[who, pl.ds(i, 1), :] for i in range(5)]
            + [coarse_source[who, pl.ds(kk, 1), :]]
            for who in range(2)
        ]

    def restricted(slot, row_ids):
        for q in range(2):
            total = field[slot, row_ids[2 * q]] + field[slot, row_ids[2 * q + 1]]
            for c in range(span // 128):
                fold[q, c] = total[:, c * 128 : (c + 1) * 128]
        sums = []
        for q in range(2):
            lines = [
                fold[q, c, pl.ds(0, depth // 2, stride=2), :]
                + fold[q, c, pl.ds(1, depth // 2, stride=2), :]
                for c in range(span // 128)
            ]
            sums.append(jnp.concatenate(lines, axis=1))
        return 0.125 * paired(*sums)

    for j in reversed(range(rows)):
        row_copies[j].wait_recv()

    last = 2 * rows - 1
    old[...] = coarse_steps(
        restricted(0, (0, 1, 2, 3)),
        restricted(0, (last, last - 1, last - 2, last - 3)),
        coarse_params(k),
        COARSE_STEPS,
        coarse_open,
        even,
    )

    for j in range(rows):
        row_copies[j].wait_send()

    for s in range(FINE_STEPS):
        now, later = s % 2, (s + 1) % 2
        reach = 2 * rows - 1 - s

        def close(j):
            given = [table[j, pl.ds(i, 1), :] for i in range(5)]
            half, rate = closure(field[now, j], *given, 1.0)
            halves[j] = half
            speeds[j] = rate

        for j in range(reach + 1):
            close(j)

        def move(j):
            heads, half = field[now, j], halves[j]
            right = fine_open * (half + shifted(half, -1, 1)) * (shifted(heads, -1, 1) - heads)
            up = (half + halves[j + 1]) * (field[now, j + 1] - heads)
            before = max(j - 1, 0)
            down = (half + halves[before]) * (field[now, before] - heads)
            balance = (
                right
                - shifted(right, 1, 1)
                + up
                + down
                + vertical(heads, half, table[j, pl.ds(5, 1), :], 1.0)
            )
            field[later, j] = heads + speeds[j] * balance

        for j in range(reach):
            move(j)

    done = FINE_STEPS % 2
    reached = restricted(done, (0, 1, 2, 3))
    chain_out[...] = (reached - old[...]) + jnp.where(has_before, 0.0, old[...])

    def chain_copy(far, who):
        return copy(
            chain_out,
            chain_in.at[k, who],
            chain_send.at[far - 1, who],
            chain_recv.at[k, who],
            (k + far, gx if who == 0 else 1 - gx, gy),
        )

    def chain_wait(kk):
        for who in range(2):
            copy(
                chain_out,
                chain_in.at[kk, who],
                chain_send.at[0, who],
                chain_recv.at[kk, who],
                partner,
            ).wait_recv()

    for far in reversed(range(1, slices)):
        @pl.when(k + far < slices)
        def _():
            for who in (1, 0):
                chain_copy(far, who).start()

    for kk in range(slices - 1):
        @pl.when(k > kk)
        def _():
            chain_wait(kk)
            if kk == 0:
                for who in range(2):
                    chained[who] = chain_in[0, who]
            else:
                moved = coarse_steps(
                    chained[0],
                    chained[1],
                    coarse_params(kk),
                    COARSE_STEPS,
                    coarse_open,
                    even,
                    both=True,
                )
                for who in range(2):
                    chained[who] = moved[who] + chain_in[kk, who]

    @pl.when(jnp.logical_not(has_before))
    def _():
        fresh[...] = old[...]

    @pl.when(has_before)
    def _():
        fresh[...] = coarse_steps(
            chained[0], chained[1], coarse_params(k), COARSE_STEPS, coarse_open, even
        )

    change = fresh[...] - old[...]
    spread_rows = (
        jnp.where(even, change, shifted(change, 1, 1)),
        jnp.where(even, shifted(change, -1, 1), change),
    )
    for q in range(2):
        for half in range(2):
            for c in range(columns // 128):
                fold[q, c, pl.ds(half, depth // 2, stride=2), :] = spread_rows[q][
                    :, c * 128 : (c + 1) * 128
                ]
    ends = [
        field[done, j, :, pl.ds(0, columns)]
        + jnp.concatenate([fold[j // 2, c] for c in range(columns // 128)], axis=1)
        for j in range(rows)
    ]
    for j in range(rows):
        out_ref[j] = jnp.where(low, ends[j], ends[rows - 1 - j])

    aux_copy.wait_send()
    for side in range(2):
        @pl.when(sends_to[side])
        def _():
            for who in range(2):
                edge_copies[side][who].wait_send()

    for far in range(1, slices):
        @pl.when(k + far < slices)
        def _():
            for who in range(2):
                chain_copy(far, who).wait_send()


def on_pair(
    sizes,
    start_heads,
    soil_class,
    soil_conductivity,
    soil_entry,
    soil_shape,
    soil_porosity,
    emitter_cell,
    emitter_plan,
    plan_rates,
):
    _, depth, rows, columns = start_heads.shape
    span = columns + EXTRA
    width = 4 * sizes["cuts"]
    vmem = pl.BlockSpec(memory_space=pltpu.VMEM)
    classes = soil_conductivity.shape
    emitters = (1, emitter_cell.shape[0])
    dma = pltpu.SemaphoreType.DMA
    f32 = jnp.float32
    half = (depth // 2, span)
    ends = pl.pallas_call(
        functools.partial(pair_kernel, dict(sizes), width),
        out_shape=jax.ShapeDtypeStruct((rows, depth, columns), f32),
        in_specs=[pl.BlockSpec(memory_space=pltpu.HBM)] * 9,
        out_specs=vmem,
        scratch_shapes=[
            pltpu.VMEM((rows, columns), jnp.int32),
            pltpu.SMEM(classes, f32),
            pltpu.SMEM(classes, f32),
            pltpu.SMEM(classes, f32),
            pltpu.SMEM(classes, f32),
            pltpu.VMEM(emitters, jnp.int32),
            pltpu.VMEM(emitters, jnp.int32),
            pltpu.VMEM(plan_rates.shape[::-1], f32),
            dma((rows + 8,)),
            pltpu.VMEM((2, 2 * rows, depth, span), f32),
            pltpu.VMEM((2 * rows, depth, span), f32),
            pltpu.VMEM((2 * rows, depth, span), f32),
            pltpu.VMEM((2 * rows, 8, span), f32),
            pltpu.VMEM((2, 8, span), f32),
            pltpu.VMEM((2, 8, span), f32),
            pltpu.VMEM((16, columns), f32),
            pltpu.VMEM((16, columns), f32),
            pltpu.VMEM((2, width + 16, EXTRA), f32),
            pltpu.VMEM((2, 2, width + 16, EXTRA), f32),
            pltpu.VMEM((2, span // 128, depth, 128), f32),
            pltpu.VMEM(half, f32),
            pltpu.VMEM(half, f32),
            pltpu.VMEM((2,) + half, f32),
            pltpu.VMEM(half, f32),
            pltpu.VMEM((sizes["cuts"], 2) + half, f32),
            dma((rows,)),
            dma((rows,)),
            dma,
            dma,
            dma((2, 2)),
            dma((2, 2)),
            dma((sizes["cuts"], 2)),
            dma((sizes["cuts"], 2)),
        ],
        compiler_params=pltpu.CompilerParams(
            collective_id=0, has_side_effects=True, vmem_limit_bytes=60 * 1024 * 1024
        ),
    )(
        start_heads,
        soil_class,
        soil_conductivity,
        soil_entry,
        soil_shape,
        soil_porosity,
        emitter_cell.reshape(1, -1),
        emitter_plan.reshape(1, -1),
        plan_rates.T,
    )
    return ends.transpose(1, 0, 2)[None]


def solution(mesh):
    in_specs = (
        P("cuts", None, "gx", "gy"),
        P("gx", "gy"),
        P(),
        P(),
        P(),
        P(),
        P(("gx", "gy")),
        P(("gx", "gy")),
        P(),
    )
    out_specs = P("cuts", None, "gx", "gy")
    sizes = mesh.shape
    fits = sizes["gx"] == 2 and sizes["cuts"] in (4, 8)
    body = functools.partial(on_pair, sizes) if fits else on_device
    return jax.shard_map(
        body, mesh=mesh, in_specs=in_specs, out_specs=out_specs, check_vma=False
    )
```

```python
import functools

import jax
import jax.numpy as jnp
from jax import lax
from jax.experimental import pallas as pl
from jax.experimental.pallas import tpu as pltpu
from jax.sharding import PartitionSpec as P

FINE_STEPS = 4
COARSE_STEPS = 2


STORAGE = 0.3


def with_halo(cells, sides, width):
    for axis, dim in sides:
        count = lax.axis_size(axis)
        ends = count - 1
        head = lax.slice_in_dim(cells, 0, width, axis=dim)
        tail = lax.slice_in_dim(cells, cells.shape[dim] - width, cells.shape[dim], axis=dim)
        cells = jnp.concatenate(
            [
                lax.ppermute(tail, axis, [(i, (i + 1) % count) for i in range(ends)]),
                cells,
                lax.ppermute(head, axis, [((i + 1) % count, i) for i in range(ends)]),
            ],
            axis=dim,
        )
    return cells


def from_behind(array, axis, by):
    length = lax.axis_size(axis)
    pairs = [(i, i + by) for i in range(length) if 0 <= i + by < length]
    return lax.ppermute(array, axis, pairs)


def conductivity(heads, saturated, entry_scale, shape_index):
    exponent = 1.0 - 1.0 / shape_index
    suction = jnp.maximum(-heads, 0.0) * entry_scale
    powered = jnp.power(suction, shape_index)
    wetted = powered / (1.0 + powered)
    return (
        saturated
        * jnp.sqrt(jnp.power(1.0 + powered, -exponent))
        * jnp.square(1.0 - jnp.power(wetted, exponent))
    )


def capacity(heads, entry_scale, shape_index, porosity):
    exponent = 1.0 - 1.0 / shape_index
    suction = jnp.maximum(-heads, 0.0) * entry_scale
    powered = jnp.power(suction, shape_index)
    return STORAGE + porosity * exponent * shape_index * entry_scale * jnp.power(
        suction, shape_index - 1.0
    ) * jnp.power(1.0 + powered, -exponent - 1.0)


def open_faces(rows, columns):
    global_row = lax.axis_index("gx") * rows + jnp.arange(rows, dtype=jnp.int32)
    global_column = lax.axis_index("gy") * columns + jnp.arange(columns, dtype=jnp.int32)
    row_total = lax.axis_size("gx") * rows
    column_total = lax.axis_size("gy") * columns
    return (
        (global_row + 1 < row_total)[None, :, None],
        (global_row > 0)[None, :, None],
        (global_column + 1 < column_total)[None, None, :],
        (global_column > 0)[None, None, :],
    )


def advance_local(
    heads, padded, conduct, conduct_pad, storage_term, source, spacing, interval, faces
):
    row_up, row_down, column_up, column_down = faces
    inverse = 1.0 / (spacing * spacing)
    flow_up = jnp.where(
        row_up,
        0.5 * (conduct + conduct_pad[:, 2:, 1:-1]) * (padded[:, 2:, 1:-1] - heads) * inverse,
        0.0,
    )
    flow_down = jnp.where(
        row_down,
        0.5 * (conduct + conduct_pad[:, :-2, 1:-1]) * (padded[:, :-2, 1:-1] - heads) * inverse,
        0.0,
    )
    balance_x = flow_up + flow_down
    flow_right = jnp.where(
        column_up,
        0.5 * (conduct + conduct_pad[:, 1:-1, 2:]) * (padded[:, 1:-1, 2:] - heads) * inverse,
        0.0,
    )
    flow_left = jnp.where(
        column_down,
        0.5 * (conduct + conduct_pad[:, 1:-1, :-2]) * (padded[:, 1:-1, :-2] - heads) * inverse,
        0.0,
    )
    balance_y = flow_right + flow_left
    downward = 0.5 * (conduct[:-1] + conduct[1:]) * ((heads[:-1] - heads[1:]) / spacing + 1.0)
    inflow = jnp.concatenate([source[None], downward], axis=0)
    outflow = jnp.concatenate([downward, conduct[-1:]], axis=0)
    balance = balance_x + balance_y + (inflow - outflow) / spacing
    return heads + interval * balance / storage_term


def run_steps(heads, params, source, faces, count, spacing, interval, is_fine):
    for s in range(count):
        conduct = conductivity(heads, params[0], params[1], params[2])
        storage_term = capacity(heads, params[1], params[2], params[3])
        stacked = jnp.stack([heads, conduct])
        if is_fine:
            stacked = with_halo(stacked, (("gx", 2), ("gy", 3)), 1)
        else:
            stacked = with_halo(stacked, (("gx", 2), ("gy", 3)), 1)
        padded = stacked[0]
        conduct_pad = stacked[1]
        heads = advance_local(
            heads, padded, conduct, conduct_pad, storage_term, source, spacing, interval, faces
        )
    return heads


def restrict(field):
    depth, rows, columns = field.shape
    return field.reshape(depth // 2, 2, rows // 2, 2, columns // 2, 2).mean(axis=(1, 3, 5))


def prolong(field):
    return jnp.repeat(jnp.repeat(jnp.repeat(field, 2, axis=0), 2, axis=1), 2, axis=2)


def coarsen_columns(params):
    count, rows, columns = params.shape
    return params.reshape(count, rows // 2, 2, columns // 2, 2).mean(axis=(2, 4))


def on_device(
    start_heads,
    soil_class,
    soil_conductivity,
    soil_entry,
    soil_shape,
    soil_porosity,
    emitter_cell,
    emitter_plan,
    plan_rates,
):
    heads_start = start_heads[0]
    depth, rows, columns = heads_start.shape
    table = jnp.stack([soil_conductivity, soil_entry, soil_shape, soil_porosity])
    classes = jnp.arange(table.shape[1], dtype=jnp.int32)
    matches = soil_class[None, :, :] == classes[:, None, None]
    params = jnp.sum(jnp.where(matches[None], table[:, :, None, None], 0.0), axis=1)
    coarse_params = coarsen_columns(params)
    plans = jnp.arange(plan_rates.shape[0], dtype=jnp.int32)
    picks = emitter_plan[:, None] == plans[None, :]
    rates_all = jnp.sum(jnp.where(picks[:, :, None], plan_rates[None], 0.0), axis=1)
    slice_total = rates_all.shape[1]
    sources = (
        jnp.zeros((slice_total, rows * columns), jnp.float32)
        .at[:, emitter_cell]
        .add(rates_all.T)
        .reshape(slice_total, rows, columns)
    )
    coarse_sources = coarsen_columns(sources)
    slice_index = lax.axis_index("cuts")
    slice_count = lax.axis_size("cuts")
    source = sources[slice_index]
    coarse_source = coarse_sources[slice_index]
    fine_open = open_faces(rows, columns)
    coarse_open = open_faces(rows // 2, columns // 2)
    fine_heads = run_steps(heads_start, params, source, fine_open, FINE_STEPS, 1.0, 1.0, True)

    def coarse_run(current, coarse_src):
        return run_steps(
            current, coarse_params, coarse_src, coarse_open, COARSE_STEPS, 2.0, 2.0, False
        )

    coarse_start = restrict(heads_start)
    coarse_old = coarse_run(coarse_start, coarse_source)
    correction = restrict(fine_heads) - coarse_old
    current = coarse_start
    coarse_new = coarse_old
    for s in range(slice_count):
        coarse_new = coarse_run(current, coarse_source)
        if s + 1 < slice_count:
            arrived = from_behind(coarse_new + correction, "cuts", 1)
            current = jnp.where(slice_index == 0, coarse_start, arrived)
    end_state = fine_heads + prolong(coarse_new - coarse_old)
    return end_state[None]


MESH = pl.DeviceIdType.MESH
EXTRA = 128


def closure(heads, entry, power, half_exponent, half_saturated, gain, interval):
    suction = jnp.maximum(-heads, 0.0) * entry
    lifted = jnp.exp(power * jnp.log(jnp.maximum(suction, 1e-37)))
    grown = 1.0 + suction * lifted
    root = jnp.exp(half_exponent * jnp.log(grown))
    wetted = lifted * root * root
    dry = 1.0 - wetted
    half_conduct = half_saturated * root * dry * dry
    rate = interval * grown / (STORAGE * grown + gain * wetted)
    return half_conduct, rate


def derived(saturated, entry, shape_index, porosity):
    power = shape_index - 1.0
    return (
        entry,
        power,
        -0.5 * power / shape_index,
        0.5 * saturated,
        porosity * power * entry,
    )


def shifted(array, by, axis):
    return pltpu.roll(array, by % array.shape[axis], axis)


def vertical(heads, half, source, spacing):
    depth = heads.shape[0]
    place = lax.broadcasted_iota(jnp.int32, heads.shape, 0)
    below = shifted(heads, -1, 0)
    flow = (half + shifted(half, -1, 0)) * ((heads - below) * (1.0 / spacing) + 1.0)
    outflow = jnp.where(place == depth - 1, 2.0 * half, flow)
    inflow = jnp.where(place == 0, source, shifted(outflow, 1, 0))
    return (inflow - outflow) * (1.0 / spacing)


def coarse_steps(own, other, params, steps, column_open, even, both=False):
    wide = 2.0
    pairs = [own, other]
    for s in range(steps):
        closed = [
            closure(pairs[w], *params[w][:5], wide) for w in range(2)
        ]
        across = jnp.where(
            even, 0.0, (closed[0][0] + closed[1][0]) * (pairs[1] - pairs[0])
        )
        fresh = []
        for w in range(2):
            if w == 1 and s == steps - 1 and not both:
                fresh.append(pairs[1])
                continue
            heads, (half, rate) = pairs[w], closed[w]
            right = column_open * (half + shifted(half, -2, 1)) * (shifted(heads, -2, 1) - heads)
            lateral = right - shifted(right, 2, 1)
            twin = jnp.where(even, shifted(heads, -1, 1), shifted(heads, 1, 1))
            twin_half = jnp.where(even, shifted(half, -1, 1), shifted(half, 1, 1))
            lateral = lateral + (half + twin_half) * (twin - heads)
            lateral = lateral + across if w == 0 else lateral - across
            balance = lateral * (1.0 / (wide * wide)) + vertical(heads, half, params[w][5], wide)
            fresh.append(heads + rate * balance)
        pairs = fresh
    return pairs if both else pairs[0]


def pair_kernel(
    sizes,
    width,
    heads_hbm,
    class_hbm,
    saturated_hbm,
    entry_hbm,
    shape_hbm,
    porosity_hbm,
    cell_hbm,
    plan_hbm,
    rates_hbm,
    out_ref,
    class_ref,
    saturated_ref,
    entry_ref,
    shape_ref,
    porosity_ref,
    cell_ref,
    plan_ref,
    rates_ref,
    load_sem,
    field,
    halves,
    speeds,
    table,
    coarse_table,
    coarse_source,
    aux_out,
    aux_in,
    edge_out,
    edge_in,
    fold,
    old,
    fresh,
    chained,
    chain_out,
    chain_in,
    row_send,
    row_recv,
    aux_send,
    aux_recv,
    edge_send,
    edge_recv,
    chain_send,
    chain_recv,
):
    slices, column_tiles = sizes["cuts"], sizes["gy"]
    _, depth, rows, columns = heads_hbm.shape
    span = columns + EXTRA
    k = lax.axis_index("cuts")
    gx = lax.axis_index("gx")
    gy = lax.axis_index("gy")
    low = gx == 0
    has_left, has_right = gy > 0, gy < column_tiles - 1
    has_before = k > 0
    pieces = 128 // width

    partner = (k, 1 - gx, gy)
    greeted = (
        (None, partner),
        (has_left, (k, gx, gy - 1)),
        (has_left, (k, 1 - gx, gy - 1)),
        (has_right, (k, gx, gy + 1)),
        (has_right, (k, 1 - gx, gy + 1)),
    ) + tuple(
        (None, (lax.rem(k + d, slices), row_half, gy))
        for d in range(1, slices)
        for row_half in (gx, 1 - gx)
    )
    barrier = pltpu.get_barrier_semaphore()
    for there, device in greeted:
        def greet(device=device):
            pl.semaphore_signal(barrier, inc=1, device_id=device, device_id_type=MESH)

        if there is None:
            greet()
        else:
            pl.when(there)(greet)

    loads = [
        pltpu.make_async_copy(
            heads_hbm.at[0, :, r, :],
            field.at[0, jnp.where(low, r, rows - 1 - r), :, pl.ds(0, columns)],
            load_sem.at[r],
        )
        for r in range(rows)
    ]
    small = [
        pltpu.make_async_copy(there, here, load_sem.at[rows + i])
        for i, (there, here) in enumerate(
            (
                (class_hbm, class_ref),
                (cell_hbm, cell_ref),
                (plan_hbm, plan_ref),
                (rates_hbm, rates_ref),
                (saturated_hbm, saturated_ref),
                (entry_hbm, entry_ref),
                (shape_hbm, shape_ref),
                (porosity_hbm, porosity_ref),
            )
        )
    ]
    for load in small + loads:
        load.start()
    for load in small:
        load.wait()
    classes = class_ref[...].astype(jnp.float32)
    for j in range(rows):
        aux_out[pl.ds(j, 1), :] = jnp.where(
            low, classes[j : j + 1], classes[rows - 1 - j : rows - j]
        )

    kinds = rates_ref.shape[1]
    plan = plan_ref[...]
    cell = cell_ref[...]
    count = plan.shape[1]
    rates_all = jnp.zeros((slices, count), jnp.float32)
    for kind in range(kinds):
        rates_all = jnp.where(plan == kind, rates_ref[:, kind : kind + 1], rates_all)
    row_of, column_of = cell // columns, cell % columns
    line = lax.broadcasted_iota(jnp.int32, (slices * rows, count), 0)
    owner, line = line // rows, line % rows
    line = jnp.where(low, line, rows - 1 - line)
    by_row = jnp.zeros((slices * rows, count), jnp.float32)
    for kk in range(slices):
        by_row = jnp.where(owner == kk, rates_all[kk : kk + 1], by_row)
    by_row = jnp.where(row_of == line, by_row, 0.0)
    by_column = jnp.where(
        column_of == lax.broadcasted_iota(jnp.int32, (columns, count), 0), 1.0, 0.0
    ).astype(jnp.bfloat16)
    parts, rest = [], by_row
    for _ in range(3):
        parts.append(rest.astype(jnp.bfloat16))
        rest = rest - parts[-1].astype(jnp.float32)
    sources = sum(
        lax.dot_general(
            part,
            by_column,
            (((1,), (1,)), ((), ())),
            preferred_element_type=jnp.float32,
        )
        for part in parts
    )
    source = sources[:rows]
    for kk in range(1, slices):
        source = jnp.where(k == kk, sources[kk * rows : (kk + 1) * rows], source)
    aux_out[pl.ds(rows, rows), :] = source
    even_own = lax.broadcasted_iota(jnp.int32, (1, columns), 1) % 2 == 0
    for kk in range(slices):
        at = [sources[kk * rows + j : kk * rows + j + 1] for j in range(rows)]
        first, second = at[0] + at[1], at[2] + at[3]
        aux_out[pl.ds(2 * rows + kk, 1), :] = 0.25 * jnp.where(
            even_own, first + shifted(first, -1, 1), second + shifted(second, 1, 1)
        )
    if slices < 8:
        aux_out[pl.ds(2 * rows + slices, 8 - slices), :] = jnp.zeros(
            (8 - slices, columns), jnp.float32
        )

    for load in loads:
        load.wait()
    lane = lax.broadcasted_iota(jnp.int32, (width, EXTRA), 1)
    packs = [jnp.zeros((width, EXTRA), jnp.float32) for _ in range(2)]
    per_row = depth // width
    for p in range(pieces):
        j, part = p // per_row, p % per_row
        here = (lane >= p * width) & (lane < (p + 1) * width)
        for side in range(2):
            block = field[0, j, pl.ds(part * width, width), pl.ds(side * (columns - 128), 128)]
            packs[side] = jnp.where(here, shifted(block, (p + side) * width, 1), packs[side])
    for side in range(2):
        edge_out[side, pl.ds(0, width), :] = packs[side]
        edge_out[side, pl.ds(width, 16), :] = aux_out[:, pl.ds(side * (columns - 128), 128)]

    def fill(side):
        for who in range(2):
            edge_in[side, who] = edge_out[side]

    pl.when(jnp.logical_not(has_right))(lambda: fill(0))
    pl.when(jnp.logical_not(has_left))(lambda: fill(1))

    beside = has_left.astype(jnp.int32) + has_right.astype(jnp.int32)
    pl.semaphore_wait(barrier, 2 * slices - 1 + 2 * beside)

    def copy(source_ref, target_ref, send, recv, device):
        return pltpu.make_async_remote_copy(
            src_ref=source_ref,
            dst_ref=target_ref,
            send_sem=send,
            recv_sem=recv,
            device_id=device,
            device_id_type=MESH,
        )

    row_copies = [
        copy(
            field.at[0, j, :, pl.ds(0, columns)],
            field.at[0, 2 * rows - 1 - j, :, pl.ds(0, columns)],
            row_send.at[j],
            row_recv.at[j],
            partner,
        )
        for j in range(rows)
    ]
    aux_copy = copy(aux_out, aux_in, aux_send, aux_recv, partner)
    edge_copies = [
        [
            copy(
                edge_out.at[side],
                edge_in.at[side, who],
                edge_send.at[side, who],
                edge_recv.at[side, who],
                (k, gx if who == 0 else 1 - gx, gy - 1 if side == 0 else gy + 1),
            )
            for who in range(2)
        ]
        for side in range(2)
    ]
    sends_to = (has_left, has_right)
    hears_from = (has_right, has_left)
    for side in range(2):
        @pl.when(sends_to[side])
        def _():
            for who in range(2):
                edge_copies[side][who].start()
    aux_copy.start()
    for j in reversed(range(rows)):
        row_copies[j].start()

    for side in range(2):
        @pl.when(hears_from[side])
        def _():
            for who in range(2):
                edge_copies[side][who].wait_recv()
    aux_copy.wait_recv()

    third = lax.broadcasted_iota(jnp.int32, (width, EXTRA), 1)
    for who in range(2):
        for p in range(pieces):
            j, part = p // per_row, p % per_row
            from_right = shifted(edge_in[0, who, pl.ds(0, width), :], -p * width, 1)
            from_left = shifted(edge_in[1, who, pl.ds(0, width), :], -(p + 1) * width, 1)
            block = jnp.where(
                third < width, from_right, jnp.where(third >= EXTRA - width, from_left, -1.0)
            )
            row = j if who == 0 else 2 * rows - 1 - j
            field[0, row, pl.ds(part * width, width), pl.ds(columns, EXTRA)] = block

    third8 = lax.broadcasted_iota(jnp.int32, (16, EXTRA), 1)
    wide_aux = [
        jnp.concatenate(
            [
                (aux_out if who == 0 else aux_in)[...],
                jnp.where(
                    third8 < EXTRA // 2,
                    edge_in[0, who, pl.ds(width, 16), :],
                    edge_in[1, who, pl.ds(width, 16), :],
                ),
            ],
            axis=1,
        )
        for who in range(2)
    ]
    lanes = lax.broadcasted_iota(jnp.int32, (1, span), 1)
    even = lanes % 2 == 0
    column = gy * columns + jnp.where(lanes < columns + EXTRA // 2, lanes, lanes - span)
    total = column_tiles * columns
    fine_open = jnp.where((column >= 0) & (column + 1 < total), 1.0, 0.0)
    coarse_open = jnp.where((column >= 0) & (column + 2 < total), 1.0, 0.0)

    def paired(first, second):
        return jnp.where(even, first + shifted(first, -1, 1), second + shifted(second, 1, 1))

    refs = (saturated_ref, entry_ref, shape_ref, porosity_ref)
    for who in range(2):
        cls = wide_aux[who]
        found = [jnp.zeros_like(cls) for _ in refs]
        for c in range(saturated_ref.shape[0]):
            match = cls == float(c)
            found = [jnp.where(match, ref[c], f) for ref, f in zip(refs, found)]
        src = wide_aux[who]
        means = [
            0.25 * paired(f[0:1] + f[1:2], f[2:3] + f[3:4]) for f in found
        ]
        coarse_source[who] = src[2 * rows :]
        for i, value in enumerate(derived(*means)):
            coarse_table[who, pl.ds(i, 1), :] = value
        for i, value in enumerate(derived(*[f[:rows] for f in found]) + (src[rows : 2 * rows],)):
            for j in range(rows):
                row = j if who == 0 else 2 * rows - 1 - j
                table[row, pl.ds(i, 1), :] = value[j : j + 1]

    def coarse_params(kk):
        return [
            [coarse_table[who, pl.ds(i, 1), :] for i in range(5)]
            + [coarse_source[who, pl.ds(kk, 1), :]]
            for who in range(2)
        ]

    def restricted(slot, row_ids):
        for q in range(2):
            total = field[slot, row_ids[2 * q]] + field[slot, row_ids[2 * q + 1]]
            for c in range(span // 128):
                fold[q, c] = total[:, c * 128 : (c + 1) * 128]
        sums = []
        for q in range(2):
            lines = [
                fold[q, c, pl.ds(0, depth // 2, stride=2), :]
                + fold[q, c, pl.ds(1, depth // 2, stride=2), :]
                for c in range(span // 128)
            ]
            sums.append(jnp.concatenate(lines, axis=1))
        return 0.125 * paired(*sums)

    last = 2 * rows - 1
    for s in range(FINE_STEPS):
        now, later = s % 2, (s + 1) % 2
        reach = 2 * rows - 1 - s

        def close(j):
            given = [table[j, pl.ds(i, 1), :] for i in range(5)]
            half, rate = closure(field[now, j], *given, 1.0)
            halves[j] = half
            speeds[j] = rate

        for j in range(reach + 1):
            if s == 0 and j >= rows:
                row_copies[2 * rows - 1 - j].wait_recv()
            close(j)

        def move(j):
            heads, half = field[now, j], halves[j]
            right = fine_open * (half + shifted(half, -1, 1)) * (shifted(heads, -1, 1) - heads)
            up = (half + halves[j + 1]) * (field[now, j + 1] - heads)
            before = max(j - 1, 0)
            down = (half + halves[before]) * (field[now, before] - heads)
            balance = (
                right
                - shifted(right, 1, 1)
                + up
                + down
                + vertical(heads, half, table[j, pl.ds(5, 1), :], 1.0)
            )
            field[later, j] = heads + speeds[j] * balance

        if s == 1:
            for j in range(rows):
                row_copies[j].wait_send()
        for j in range(reach):
            move(j)
        if s == 0:
            chained[0] = restricted(0, (0, 1, 2, 3))
            chained[1] = restricted(0, (last, last - 1, last - 2, last - 3))


    done = FINE_STEPS % 2
    reached = restricted(done, (0, 1, 2, 3))

    def chain_copy(far, who):
        return copy(
            chain_out,
            chain_in.at[k, who],
            chain_send.at[far - 1, who],
            chain_recv.at[k, who],
            (k + far, gx if who == 0 else 1 - gx, gy),
        )

    def chain_wait(kk):
        for who in range(2):
            copy(
                chain_out,
                chain_in.at[kk, who],
                chain_send.at[0, who],
                chain_recv.at[kk, who],
                partner,
            ).wait_recv()

    @pl.when(jnp.logical_not(has_before))
    def _():
        chain_out[...] = reached
        for far in reversed(range(1, slices)):
            for who in (1, 0):
                chain_copy(far, who).start()

    old[...] = coarse_steps(
        chained[0], chained[1], coarse_params(k), COARSE_STEPS, coarse_open, even
    )

    @pl.when(has_before)
    def _():
        chain_out[...] = reached - old[...]

    for far in reversed(range(1, slices)):
        @pl.when(has_before & (k + far < slices))
        def _():
            for who in (1, 0):
                chain_copy(far, who).start()

    for kk in range(slices - 1):
        @pl.when(k > kk)
        def _():
            chain_wait(kk)
            if kk == 0:
                for who in range(2):
                    chained[who] = chain_in[0, who]
            else:
                moved = coarse_steps(
                    chained[0],
                    chained[1],
                    coarse_params(kk),
                    COARSE_STEPS,
                    coarse_open,
                    even,
                    both=True,
                )
                for who in range(2):
                    chained[who] = moved[who] + chain_in[kk, who]

    @pl.when(jnp.logical_not(has_before))
    def _():
        fresh[...] = old[...]

    @pl.when(has_before)
    def _():
        fresh[...] = coarse_steps(
            chained[0], chained[1], coarse_params(k), COARSE_STEPS, coarse_open, even
        )

    change = fresh[...] - old[...]
    spread_rows = (
        jnp.where(even, change, shifted(change, 1, 1)),
        jnp.where(even, shifted(change, -1, 1), change),
    )
    for q in range(2):
        for half in range(2):
            for c in range(columns // 128):
                fold[q, c, pl.ds(half, depth // 2, stride=2), :] = spread_rows[q][
                    :, c * 128 : (c + 1) * 128
                ]
    ends = [
        field[done, j, :, pl.ds(0, columns)]
        + jnp.concatenate([fold[j // 2, c] for c in range(columns // 128)], axis=1)
        for j in range(rows)
    ]
    for j in range(rows):
        out_ref[j] = jnp.where(low, ends[j], ends[rows - 1 - j])

    aux_copy.wait_send()
    for side in range(2):
        @pl.when(sends_to[side])
        def _():
            for who in range(2):
                edge_copies[side][who].wait_send()

    for far in range(1, slices):
        @pl.when(k + far < slices)
        def _():
            for who in range(2):
                chain_copy(far, who).wait_send()


def on_pair(
    sizes,
    start_heads,
    soil_class,
    soil_conductivity,
    soil_entry,
    soil_shape,
    soil_porosity,
    emitter_cell,
    emitter_plan,
    plan_rates,
):
    _, depth, rows, columns = start_heads.shape
    span = columns + EXTRA
    width = 4 * sizes["cuts"]
    vmem = pl.BlockSpec(memory_space=pltpu.VMEM)
    classes = soil_conductivity.shape
    emitters = (1, emitter_cell.shape[0])
    dma = pltpu.SemaphoreType.DMA
    f32 = jnp.float32
    half = (depth // 2, span)
    ends = pl.pallas_call(
        functools.partial(pair_kernel, dict(sizes), width),
        out_shape=jax.ShapeDtypeStruct((rows, depth, columns), f32),
        in_specs=[pl.BlockSpec(memory_space=pltpu.HBM)] * 9,
        out_specs=vmem,
        scratch_shapes=[
            pltpu.VMEM((rows, columns), jnp.int32),
            pltpu.SMEM(classes, f32),
            pltpu.SMEM(classes, f32),
            pltpu.SMEM(classes, f32),
            pltpu.SMEM(classes, f32),
            pltpu.VMEM(emitters, jnp.int32),
            pltpu.VMEM(emitters, jnp.int32),
            pltpu.VMEM(plan_rates.shape[::-1], f32),
            dma((rows + 8,)),
            pltpu.VMEM((2, 2 * rows, depth, span), f32),
            pltpu.VMEM((2 * rows, depth, span), f32),
            pltpu.VMEM((2 * rows, depth, span), f32),
            pltpu.VMEM((2 * rows, 8, span), f32),
            pltpu.VMEM((2, 8, span), f32),
            pltpu.VMEM((2, 8, span), f32),
            pltpu.VMEM((16, columns), f32),
            pltpu.VMEM((16, columns), f32),
            pltpu.VMEM((2, width + 16, EXTRA), f32),
            pltpu.VMEM((2, 2, width + 16, EXTRA), f32),
            pltpu.VMEM((2, span // 128, depth, 128), f32),
            pltpu.VMEM(half, f32),
            pltpu.VMEM(half, f32),
            pltpu.VMEM((2,) + half, f32),
            pltpu.VMEM(half, f32),
            pltpu.VMEM((sizes["cuts"], 2) + half, f32),
            dma((rows,)),
            dma((rows,)),
            dma,
            dma,
            dma((2, 2)),
            dma((2, 2)),
            dma((sizes["cuts"], 2)),
            dma((sizes["cuts"], 2)),
        ],
        compiler_params=pltpu.CompilerParams(
            collective_id=0, has_side_effects=True, vmem_limit_bytes=60 * 1024 * 1024
        ),
    )(
        start_heads,
        soil_class,
        soil_conductivity,
        soil_entry,
        soil_shape,
        soil_porosity,
        emitter_cell.reshape(1, -1),
        emitter_plan.reshape(1, -1),
        plan_rates.T,
    )
    return ends.transpose(1, 0, 2)[None]


def solution(mesh):
    in_specs = (
        P("cuts", None, "gx", "gy"),
        P("gx", "gy"),
        P(),
        P(),
        P(),
        P(),
        P(("gx", "gy")),
        P(("gx", "gy")),
        P(),
    )
    out_specs = P("cuts", None, "gx", "gy")
    sizes = mesh.shape
    fits = sizes["gx"] == 2 and sizes["cuts"] in (4, 8)
    body = functools.partial(on_pair, sizes) if fits else on_device
    return jax.shard_map(
        body, mesh=mesh, in_specs=in_specs, out_specs=out_specs, check_vma=False
    )
```
